256 devices in a mesh: dp: 32 (over z, y), tensor: 8 (over x, core).
Axes of the slice: x: 4, y: 4, z: 8, core: 2. Of those that a mesh axis runs over, the one named last changes fastest.
Arguments:
- context: bfloat16 [65536, 8192], P('dp', 'tensor'), may hold values from -0.3125 to 0.3125
- out_grad: bfloat16 [65536, 1024], P(('dp', 'tensor')), may hold values from -6 to 6
- out_weight: bfloat16 [8192, 1024], P('tensor'), may hold values from -0.1875 to 0.1875
- error: bfloat16 [32, 8192, 1024], P('dp', 'tensor'), may hold values from -23 to 23
- q_init: float32 [1024, 64], replicated, may hold values from -6 to 6
Outputs:
- ctx_grad: bfloat16 [65536, 8192], P('dp', 'tensor')
- new_error: bfloat16 [32, 8192, 1024], P('dp', 'tensor')
- q_factor: float32 [1024, 64], replicated
The draws below stay inside these ranges and needn't reach their ends.
All inputs are finite; a program needn't handle non-finite values.
Results may differ from the reference program's by a relative error of at most 0.0085.
Values may be sent and summed in bfloat16 or wider, within the bound.
A program may use at most 64 MiB of HBM per device.

```python
import math
import jax
import jax.numpy as jnp
from jax import lax

D = 1024
RANK = 64
INNER = 8192
TOKENS = 2048
ALL_TOKENS = 65536
N_DP = 32


def draw_error(key, part):
    key = jax.random.fold_in(key, 7)
    key_rows, key_cols, key_base = jax.random.split(key, 3)
    position = jnp.arange(INNER, dtype=jnp.float32) / max(INNER - 1, 1)
    replica = jnp.arange(N_DP, dtype=jnp.float32) / max(N_DP - 1, 1)
    rise = (3.0 ** position)[None, :, None] * (3.0 ** replica)[:, None, None]
    rows = rise * jnp.exp(jax.random.uniform(key_rows, (N_DP, INNER, 1), jnp.float32) * math.log(3.0))
    cols = jnp.exp(jax.random.uniform(key_cols, (1, 1, D), jnp.float32) * math.log(10.0))
    base = jax.random.uniform(key_base, (N_DP, INNER, D), jnp.float32, -1.7, 1.7)
    value = 0.05 * base * rows * cols
    return value.astype(jnp.bfloat16)


def block_levels(rng, dims, pieces, least, top_value):
    factor_of, own = 1.0, jax.random.fold_in(rng, 6)
    for dim, parts in pieces:
        draws = jnp.exp(jax.random.uniform(jax.random.fold_in(own, dim), (parts,), jnp.float32, least / len(pieces), top_value / len(pieces)))
        factor_of = factor_of * jnp.repeat(draws, dims[dim] // parts).reshape([-1 if axis == dim else 1 for axis in range(len(dims))])
    return factor_of


def bell_draw(key, shape, scale, reach, pieces=(), kind=jnp.bfloat16):
    values = jax.random.normal(key, shape, jnp.float32) * scale
    if len(pieces) > 0:
        values = block_levels(key, shape, pieces, -0.22, 0.18) * values
    return jnp.clip(values, min=-reach, max=reach).astype(kind)


def setup_inputs(seed: int = 0) -> dict:
    arg_keys = jax.random.split(jax.random.key(seed), 6)
    context = bell_draw(arg_keys[0], (ALL_TOKENS, INNER), (TOKENS ** -0.5), 0.3125, ((0, 32), (1, 8)))
    out_grad = bell_draw(arg_keys[1], (ALL_TOKENS, D), 1.0, 6.0, ((0, 256),))
    out_weight = bell_draw(arg_keys[2], (INNER, D), D ** -0.5, 0.1875, ((0, 8),))
    error = draw_error(jax.random.fold_in(arg_keys[5], 71), 0)
    q_init = bell_draw(arg_keys[4], (D, RANK), 1.0, 6.0, (), jnp.float32)
    return dict(context=context, out_grad=out_grad, out_weight=out_weight, error=error, q_init=q_init)


HIGH = lax.Precision.HIGHEST

def reference(context, out_grad, out_weight, error, q_init):
    ctx_grad = jnp.dot(out_grad.astype(jnp.float32), out_weight.T.astype(jnp.float32), preferred_element_type=jnp.float32).astype(jnp.bfloat16)
    ctx_blocks = context.reshape(N_DP, TOKENS, INNER)
    dy_blocks = out_grad.reshape(N_DP, TOKENS, D)

    def grad_of(pair):
        return jnp.dot(pair[0].T.astype(jnp.float32), pair[1].astype(jnp.float32), preferred_element_type=jnp.float32).astype(jnp.bfloat16)
    grads = lax.map(grad_of, (ctx_blocks, dy_blocks))

    def p_of(pair):
        merged = pair[0].astype(jnp.float32) + pair[1].astype(jnp.float32)
        return jnp.dot(merged, q_init, precision=HIGH)
    p_mean = jnp.sum(lax.map(p_of, (grads, error)), axis=0) / N_DP
    gram = jnp.dot(p_mean.T, p_mean, precision=HIGH)
    chol = jnp.linalg.cholesky(gram)
    p_factor = jax.scipy.linalg.solve_triangular(chol, p_mean.T, lower=True).T

    def q_of(pair):
        merged = pair[0].astype(jnp.float32) + pair[1].astype(jnp.float32)
        return jnp.dot(merged.T, p_factor, precision=HIGH)
    q_factor = jnp.sum(lax.map(q_of, (grads, error)), axis=0) / N_DP

    def residue(pair):
        merged = pair[0].astype(jnp.float32) + pair[1].astype(jnp.float32)
        return (merged - jnp.dot(p_factor, q_factor.T, precision=HIGH)).astype(jnp.bfloat16)
    new_error = lax.map(residue, (grads, error))
    return (ctx_grad, new_error, q_factor)
```

```python
import functools

import jax
import jax.numpy as jnp
from jax import lax
from jax.experimental import pallas as pl
from jax.experimental.pallas import tpu as pltpu
from jax.sharding import PartitionSpec as P

MESH = pl.DeviceIdType.MESH
F32 = jnp.float32
BF16 = jnp.bfloat16
NX = 4
RANK = 64
BLOCKS = 4
NT = (((1,), (1,)), ((), ()))
NN = (((1,), (0,)), ((), ()))


def dot(a, b, dims=NN):
    return lax.dot_general(a, b, dims, preferred_element_type=F32)


def split(v):
    hi = v.astype(BF16)
    return hi, (v - hi.astype(F32)).astype(BF16)


def eliminate(a, first, last):
    row_ids = lax.broadcasted_iota(jnp.int32, a.shape, 0)
    for k in range(first, last):
        col = jnp.broadcast_to(a[:, k : k + 1], a.shape)
        row = a[k : k + 1, :] / col[k : k + 1, :]
        a = a - jnp.where(row_ids > k, col, 0.0) * row
    return a


def kernel(
    ny, nz,
    ctx_hbm, dy_hbm, w_hbm, e_hbm, q_hbm,
    dctx_hbm, ne_hbm, qf_hbm,
    cv, ct, og, wv, ev, qv, q2, yg, pe, gb, ps, prx, pall, pt,
    gx1, gx2, aug, ze, zs, z1, z2, zall, ft, qs, cs, ns, qo,
    load, store, y_send, y_near, y_sib, o_send, o_left, o_right, o_far, o_sib,
    p_send, p_recv, g_send, g_recv, z_send, z_recv,
):
    dp, ten = lax.axis_index("dp"), lax.axis_index("tensor")
    z, y = dp // ny, dp % ny
    x, core = ten // 2, ten % 2
    ndp, nten = ny * nz, 2 * NX
    nplane = ny * nten
    rows = dy_hbm.shape[0]
    half = rows // 2
    tokens = rows * nten
    width = og.shape[2]
    inner, d = w_hbm.shape
    xl, xr, xo = lax.rem(x + NX - 1, NX), lax.rem(x + 1, NX), lax.rem(x + 2, NX)
    sib = {"tensor": 2 * x + 1 - core}
    left, right, far = ({"tensor": 2 * i + core} for i in (xl, xr, xo))

    barrier = pltpu.get_barrier_semaphore()

    @pl.loop(1, nten)
    def _(j):
        pl.semaphore_signal(barrier, inc=1, device_id={"tensor": lax.rem(ten + j, nten)}, device_id_type=MESH)

    @pl.loop(1, ndp)
    def _(j):
        pl.semaphore_signal(barrier, inc=1, device_id={"dp": lax.rem(dp + j, ndp)}, device_id_type=MESH)

    def piece(b, owner, part=None):
        if part is None:
            return og.at[b, pl.ds(pl.multiple_of(owner * rows, rows), rows)]
        return og.at[b, pl.ds(pl.multiple_of(owner * rows + part * half, half), half)]

    def send(src, dst, s_sem, r_sem, dev):
        pltpu.make_async_remote_copy(
            src_ref=src, dst_ref=dst, send_sem=s_sem, recv_sem=r_sem, device_id=dev, device_id_type=MESH
        ).start()

    def await_bytes(ref, sem):
        pltpu.make_async_copy(ref, ref, sem).wait()

    loads = []
    for b in range(BLOCKS):
        loads.append(pltpu.make_async_copy(dy_hbm.at[:, pl.ds(b * width, width)], piece(b, ten), load.at[b]))
    load_q = pltpu.make_async_copy(q_hbm, qv, load.at[BLOCKS])
    load_e = pltpu.make_async_copy(e_hbm.at[0], ev, load.at[BLOCKS + 1])
    load_c = pltpu.make_async_copy(ctx_hbm, cv, load.at[BLOCKS + 2])
    load_w = pltpu.make_async_copy(w_hbm, wv, load.at[BLOCKS + 3])
    for c in [load_q, *loads, load_e, load_c, load_w]:
        c.start()

    load_q.wait()
    hi, lo = split(qv[...].T)
    q2[0:RANK] = hi
    q2[RANK : 2 * RANK] = lo
    for c in loads:
        c.wait()
    yv = jnp.zeros((2 * RANK, rows), F32)
    own = pl.ds(pl.multiple_of(ten * rows, rows), rows)
    for b in range(BLOCKS):
        yv += dot(q2[:, b * width : (b + 1) * width], og[b, own, :], NT)
    yg[ten] = (yv[:RANK] + yv[RANK:]).astype(BF16)

    pl.semaphore_wait(barrier, nten - 1 + ndp - 1)

    for dev in (right, left, far):
        send(yg.at[ten], yg.at[ten], y_send, y_near, dev)
    send(yg.at[ten], yg.at[ten], y_send, y_sib, sib)

    def send_own(b):
        mine = piece(b, ten)
        send(mine, mine, o_send.at[b], o_left.at[b], right)
        send(mine, mine, o_send.at[b], o_right.at[b], left)
        send(mine, mine, o_send.at[b], o_sib.at[b], sib)

    def pass_near(b):
        from_left, from_right = piece(b, 2 * xl + core), piece(b, 2 * xr + core)
        await_bytes(from_left, o_left.at[b])
        onward = piece(b, 2 * xl + core, 0)
        send(onward, onward, o_send.at[b], o_far.at[b], right)
        send(from_left, from_left, o_send.at[b], o_sib.at[b], sib)
        await_bytes(from_right, o_right.at[b])
        onward = piece(b, 2 * xr + core, 1)
        send(onward, onward, o_send.at[b], o_far.at[b], left)
        send(from_right, from_right, o_send.at[b], o_sib.at[b], sib)

    def pass_far(b):
        from_far = piece(b, 2 * xo + core)
        await_bytes(from_far, o_far.at[b])
        send(from_far, from_far, o_send.at[b], o_sib.at[b], sib)

    def grad_block(b):
        await_bytes(og.at[b, pl.ds(0, rows * NX)], o_sib.at[b])
        mt = min(512, inner)

        @pl.loop(0, inner // mt)
        def _(i):
            r = pl.ds(pl.multiple_of(i * mt, mt), mt)
            gb[r, b * width : (b + 1) * width] = dot(ct[r, :], og[b]).astype(BF16)

    send_own(0)
    send_own(1)

    load_e.wait()
    for n in range(4):
        r = slice(n * inner // 4, (n + 1) * inner // 4)
        v = dot(q2[...], ev[r, :], NT)
        pe[:, r] = v[:RANK] + v[RANK:]
    load_c.wait()
    for t in range(nten):
        ct[:, t * rows : (t + 1) * rows] = cv[t * rows : (t + 1) * rows, :].T

    await_bytes(yg.at[pl.ds(0, 3)], y_near)
    for i in (xl, xr, xo):
        got = yg.at[2 * i + core]
        send(got, got, y_send, y_sib, sib)
    await_bytes(yg.at[pl.ds(0, 4)], y_sib)

    pv = pe[...]
    for t in range(nten):
        pv += dot(yg[t], cv[t * rows : (t + 1) * rows, :])
    pr, pc = RANK // ny, inner // nz
    pv = pv.astype(BF16)
    for k in range(ndp):
        ps[k] = pv[(k % ny) * pr : (k % ny + 1) * pr, (k // ny) * pc : (k // ny + 1) * pc]

    @pl.loop(1, ndp)
    def _(j):
        to = lax.rem(dp + j, ndp)
        send(ps.at[to], prx.at[dp], p_send.at[0], p_recv.at[0], {"dp": to})

    prx[dp] = ps[dp]
    pass_near(0)
    send_own(2)

    await_bytes(prx.at[pl.ds(0, ndp - 1)], p_recv.at[0])
    total = prx[0].astype(F32)
    for k in range(1, ndp):
        total += prx[k].astype(F32)
    pall[dp] = (total * (1.0 / ndp)).astype(BF16)

    @pl.loop(1, ndp)
    def _(j):
        send(pall.at[dp], pall.at[dp], p_send.at[1], p_recv.at[1], {"dp": lax.rem(dp + j, ndp)})

    pass_near(1)
    send_own(3)
    pass_far(0)
    grad_block(0)

    await_bytes(pall.at[pl.ds(0, ndp - 1)], p_recv.at[1])
    for k in range(ndp):
        pt[(k % ny) * pr : (k % ny + 1) * pr, (k // ny) * pc : (k // ny + 1) * pc] = pall[k]
    gram = dot(pt[...], pt[...], NT)
    gx1[core] = jnp.concatenate([gram[: RANK // 2], gram[RANK // 2 :]], axis=1)
    send(gx1.at[core], gx1.at[core], g_send.at[0], g_recv.at[0], sib)
    pass_far(1)
    pass_near(2)
    ze[...] = dot(pt[...], ev[...])
    await_bytes(gx1.at[0], g_recv.at[0])
    gx2[x] = gx1[0] + gx1[1]
    for dev in (right, left, far):
        send(gx2.at[x], gx2.at[x], g_send.at[1], g_recv.at[1], dev)
    grad_block(1)
    pass_near(3)
    pass_far(2)

    await_bytes(gx2.at[pl.ds(0, NX - 1)], g_recv.at[1])
    gram = gx2[0] + gx2[1] + gx2[2] + gx2[3]
    gram = jnp.concatenate([gram[:, :RANK], gram[:, RANK:]], axis=0)
    eye = (
        lax.broadcasted_iota(jnp.int32, (RANK, RANK), 0) == lax.broadcasted_iota(jnp.int32, (RANK, RANK), 1)
    ).astype(F32)
    aug[...] = eliminate(jnp.concatenate([gram, eye], axis=1), 0, 24)
    grad_block(2)
    pass_far(3)
    grad_block(3)

    zv = ze[...] + dot(pt[...], gb[...])
    zr, zc = RANK // ny, d // nten
    for k in range(nplane):
        zs[k] = zv[(k % ny) * zr : (k % ny + 1) * zr, (k // ny) * zc : (k // ny + 1) * zc]
    me = ten * ny + y

    @pl.loop(1, nplane)
    def _(j):
        to = lax.rem(me + j, nplane)
        send(zs.at[to], z1.at[me], z_send.at[0], z_recv.at[0], {"dp": z * ny + to % ny, "tensor": to // ny})

    z1[me] = zs[me]

    load_w.wait()
    out_rows = tokens // 4

    def ctx_chunk(i):
        r = pl.ds(i * out_rows, out_rows)
        for n in range(4):
            c = slice(n * inner // 4, (n + 1) * inner // 4)
            acc = dot(og[0, r, :], wv[c, 0:width], NT)
            for b in range(1, BLOCKS):
                acc += dot(og[b, r, :], wv[c, b * width : (b + 1) * width], NT)
            cs[r, c] = acc.astype(BF16)
        out = pltpu.make_async_copy(cs.at[r], dctx_hbm.at[r], store.at[i])
        out.start()
        return out

    outs = [ctx_chunk(0), ctx_chunk(1)]

    await_bytes(z1.at[pl.ds(0, nplane - 1)], z_recv.at[0])
    total = z1[0]
    for k in range(1, nplane):
        total += z1[k]
    z2[z] = total

    @pl.loop(1, nz)
    def _(j):
        to = lax.rem(z + j, nz)
        send(z2.at[z], z2.at[z], z_send.at[1], z_recv.at[1], {"dp": to * ny + y})

    a = eliminate(aug[...], 24, RANK)
    on_diag = lax.broadcasted_iota(jnp.int32, (RANK, RANK), 0) == lax.broadcasted_iota(jnp.int32, (RANK, RANK), 1)
    diag = jnp.sum(jnp.where(on_diag, a[:, :RANK], 0.0), axis=1, keepdims=True)
    inv = a[:, RANK:] / jnp.sqrt(diag)
    inv_hi, inv_lo = split(inv)
    f = dot(inv_hi, pt[...]) + dot(inv_lo, pt[...])
    f_hi, f_lo = split(f)
    ft[...] = jnp.concatenate([f_hi, f_lo, f_hi], axis=0).T

    await_bytes(z2.at[pl.ds(0, nz - 1)], z_recv.at[1])
    total = z2[0]
    for k in range(1, nz):
        total += z2[k]
    zall[me] = total * (1.0 / ndp)

    @pl.loop(1, nplane)
    def _(j):
        to = lax.rem(me + j, nplane)
        send(zall.at[me], zall.at[me], z_send.at[2], z_recv.at[2], {"dp": z * ny + to % ny, "tensor": to // ny})

    outs += [ctx_chunk(2), ctx_chunk(3)]

    await_bytes(zall.at[pl.ds(0, nplane - 1)], z_recv.at[2])
    for k in range(nplane):
        hi, lo = split(zall[k])
        r, c = (k % ny) * zr, slice((k // ny) * zc, (k // ny + 1) * zc)
        qs[r : r + zr, c] = hi
        qs[RANK + r : RANK + r + zr, c] = hi
        qs[2 * RANK + r : 2 * RANK + r + zr, c] = lo
    qt = dot(jnp.concatenate([inv_hi, inv_lo, inv_hi], axis=1), qs[...])
    qo[...] = qt.T
    out = pltpu.make_async_copy(qo, qf_hbm, store.at[4])
    out.start()
    outs.append(out)
    hi, lo = split(qt)
    qs[0:RANK] = hi
    qs[RANK : 2 * RANK] = hi
    qs[2 * RANK : 3 * RANK] = lo
    ne_rows = inner // 4
    for i in range(4):
        r = pl.ds(i * ne_rows, ne_rows)
        low = dot(ft[r, :], qs[...])
        ns[r, :] = (gb[r, :].astype(F32) + ev[r, :].astype(F32) - low).astype(BF16)
        out = pltpu.make_async_copy(ns.at[r], ne_hbm.at[0, r], store.at[5 + i])
        out.start()
        outs.append(out)

    await_bytes(yg.at[pl.ds(0, 7)], y_send)
    for b in range(BLOCKS):
        await_bytes(og.at[b, pl.ds(0, 7 * rows)], o_send.at[b])
    await_bytes(prx.at[pl.ds(0, ndp - 1)], p_send.at[0])
    await_bytes(pall.at[pl.ds(0, ndp - 1)], p_send.at[1])
    await_bytes(gx1.at[0], g_send.at[0])
    await_bytes(gx2.at[pl.ds(0, NX - 1)], g_send.at[1])
    await_bytes(z1.at[pl.ds(0, nplane - 1)], z_send.at[0])
    await_bytes(z2.at[pl.ds(0, nz - 1)], z_send.at[1])
    await_bytes(zall.at[pl.ds(0, nplane - 1)], z_send.at[2])
    for out in outs:
        out.wait()


def shards(ny, nz, context, out_grad, out_weight, error, q_init):
    tokens, inner = context.shape
    rows, d = out_grad.shape
    ndp, nplane = ny * nz, 2 * NX * ny
    width = d // BLOCKS
    dma = pltpu.SemaphoreType.DMA
    any_ = pl.BlockSpec(memory_space=pl.ANY)
    pr, pc = RANK // ny, inner // nz
    zr, zc = RANK // ny, d // (2 * NX)
    vm = pltpu.VMEM
    return pl.pallas_call(
        functools.partial(kernel, ny, nz),
        out_shape=(
            jax.ShapeDtypeStruct((tokens, inner), BF16),
            jax.ShapeDtypeStruct((1, inner, d), BF16),
            jax.ShapeDtypeStruct((d, RANK), F32),
        ),
        in_specs=[any_] * 5,
        out_specs=(any_, any_, any_),
        scratch_shapes=[
            vm((tokens, inner), BF16),
            vm((inner, tokens), BF16),
            vm((BLOCKS, tokens, width), BF16),
            vm((inner, d), BF16),
            vm((inner, d), BF16),
            vm((d, RANK), F32),
            vm((2 * RANK, d), BF16),
            vm((2 * NX, RANK, rows), BF16),
            vm((RANK, inner), F32),
            vm((inner, d), BF16),
            vm((ndp, pr, pc), BF16),
            vm((ndp, pr, pc), BF16),
            vm((ndp, pr, pc), BF16),
            vm((RANK, inner), BF16),
            vm((2, RANK // 2, 2 * RANK), F32),
            vm((NX, RANK // 2, 2 * RANK), F32),
            vm((RANK, 2 * RANK), F32),
            vm((RANK, d), F32),
            vm((nplane, zr, zc), F32),
            vm((nplane, zr, zc), F32),
            vm((nz, zr, zc), F32),
            vm((nplane, zr, zc), F32),
            vm((inner, 3 * RANK), BF16),
            vm((3 * RANK, d), BF16),
            vm((tokens, inner), BF16),
            vm((inner, d), BF16),
            vm((d, RANK), F32),
            dma((BLOCKS + 4,)),
            dma((9,)),
            dma, dma, dma,
            dma((BLOCKS,)), dma((BLOCKS,)), dma((BLOCKS,)), dma((BLOCKS,)), dma((BLOCKS,)),
            dma((2,)), dma((2,)), dma((2,)), dma((2,)), dma((3,)), dma((3,)),
        ],
        compiler_params=pltpu.CompilerParams(
            collective_id=0, has_side_effects=True, vmem_limit_bytes=56 * 2**20
        ),
    )(context, out_grad, out_weight, error, q_init)


def solution(mesh):
    ndp = mesh.shape["dp"]
    ny = 4 if ndp % 4 == 0 else 1
    placed = (
        P("dp", "tensor"),
        P(("dp", "tensor"), None),
        P("tensor", None),
        P("dp", "tensor", None),
        P(),
    )
    return jax.shard_map(
        functools.partial(shards, ny, ndp // ny),
        mesh=mesh,
        in_specs=placed,
        out_specs=(P("dp", "tensor"), P("dp", "tensor", None), P()),
        check_vma=False,
    )
```

```python
import functools

import jax
import jax.numpy as jnp
from jax import lax
from jax.experimental import pallas as pl
from jax.experimental.pallas import tpu as pltpu
from jax.sharding import PartitionSpec as P

MESH = pl.DeviceIdType.MESH
F32 = jnp.float32
BF16 = jnp.bfloat16
NX = 4
RANK = 64
BLOCKS = 4
NT = (((1,), (1,)), ((), ()))
NN = (((1,), (0,)), ((), ()))


def dot(a, b, dims=NN):
    return lax.dot_general(a, b, dims, preferred_element_type=F32)


def split(v):
    hi = v.astype(BF16)
    return hi, (v - hi.astype(F32)).astype(BF16)


def eliminate(a, first, last):
    row_ids = lax.broadcasted_iota(jnp.int32, a.shape, 0)
    for k in range(first, last, 2):
        c0 = jnp.broadcast_to(a[:, k : k + 1], a.shape)
        c1 = jnp.broadcast_to(a[:, k + 1 : k + 2], a.shape)
        r0, r1 = a[k : k + 1, :], a[k + 1 : k + 2, :]
        aa, bb, cc = c0[k : k + 1, :], c0[k + 1 : k + 2, :], c1[k + 1 : k + 2, :]
        inv = 1.0 / (aa * cc - bb * bb)
        w0 = (cc * r0 - bb * r1) * inv
        w1 = (aa * r1 - bb * r0) * inv
        second = r1 - (bb / aa) * r0
        below = a - c0 * w0 - c1 * w1
        a = jnp.where(row_ids > k + 1, below, jnp.where(row_ids == k + 1, second, a))
    return a


def kernel(
    ny, nz,
    ctx_hbm, dy_hbm, w_hbm, e_hbm, q_hbm,
    cs, gb, ev, ft, lf, zq,
    cv, ct, og, wv, qv, q2, yg, pe, ps, prx, pall, pt,
    gx1, gx2, aug, ze, zs, z1, z2, zall,
    load, y_send, y_near, y_sib, o_send, o_left, o_right, o_far, o_sib,
    p_send, p_recv, g_send, g_recv, z_send, z_recv,
):
    dp, ten = lax.axis_index("dp"), lax.axis_index("tensor")
    z, y = dp // ny, dp % ny
    x, core = ten // 2, ten % 2
    ndp, nten = ny * nz, 2 * NX
    nplane = ny * nten
    rows = dy_hbm.shape[0]
    half = rows // 2
    tokens = rows * nten
    width = og.shape[2]
    inner, d = w_hbm.shape
    xl, xr, xo = lax.rem(x + NX - 1, NX), lax.rem(x + 1, NX), lax.rem(x + 2, NX)
    sib = {"tensor": 2 * x + 1 - core}
    left, right, far = ({"tensor": 2 * i + core} for i in (xl, xr, xo))

    barrier = pltpu.get_barrier_semaphore()

    @pl.loop(1, nten)
    def _(j):
        pl.semaphore_signal(barrier, inc=1, device_id={"tensor": jnp.where(ten + j >= nten, ten + j - nten, ten + j)}, device_id_type=MESH)

    @pl.loop(1, ndp)
    def _(j):
        pl.semaphore_signal(barrier, inc=1, device_id={"dp": jnp.where(dp + j >= ndp, dp + j - ndp, dp + j)}, device_id_type=MESH)

    def piece(b, owner, part=None):
        if part is None:
            return og.at[b, pl.ds(pl.multiple_of(owner * rows, rows), rows)]
        return og.at[b, pl.ds(pl.multiple_of(owner * rows + part * half, half), half)]

    def send(src, dst, s_sem, r_sem, dev):
        pltpu.make_async_remote_copy(
            src_ref=src, dst_ref=dst, send_sem=s_sem, recv_sem=r_sem, device_id=dev, device_id_type=MESH
        ).start()

    def wrap(i, n):
        return jnp.where(i >= n, i - n, i)

    def each_replica(act):
        for j in range(1, ny):
            to_y = wrap(y + j, ny)
            act(z * ny + to_y, {"dp": z * ny + to_y})

        @pl.loop(1, nz)
        def _(i):
            to_z = wrap(z + i, nz)
            for j in range(ny):
                to = to_z * ny + wrap(y + j, ny)
                act(to, {"dp": to})

    def each_in_plane(act):
        for j in range(1, ny):
            to_y = wrap(y + j, ny)
            act(ten * ny + to_y, {"dp": z * ny + to_y})

        @pl.loop(1, nten)
        def _(i):
            to_t = wrap(ten + i, nten)
            for j in range(ny):
                to_y = wrap(y + j, ny)
                act(to_t * ny + to_y, {"dp": z * ny + to_y, "tensor": to_t})

    def await_bytes(ref, sem):
        pltpu.make_async_copy(ref, ref, sem).wait()

    loads = []
    for b in range(BLOCKS):
        loads.append(pltpu.make_async_copy(dy_hbm.at[:, pl.ds(b * width, width)], piece(b, ten), load.at[b]))
    load_q = pltpu.make_async_copy(q_hbm, qv, load.at[BLOCKS])
    load_e = pltpu.make_async_copy(e_hbm.at[0], ev, load.at[BLOCKS + 1])
    load_c = pltpu.make_async_copy(ctx_hbm, cv, load.at[BLOCKS + 2])
    load_w = pltpu.make_async_copy(w_hbm, wv, load.at[BLOCKS + 3])
    for c in [load_q, *loads, load_e, load_c, load_w]:
        c.start()

    load_q.wait()
    hi, lo = split(qv[...])
    q2[0:RANK] = hi
    q2[RANK : 2 * RANK] = lo
    for c in loads:
        c.wait()
    yv = jnp.zeros((2 * RANK, rows), F32)
    own = pl.ds(pl.multiple_of(ten * rows, rows), rows)
    for b in range(BLOCKS):
        yv += dot(q2[:, b * width : (b + 1) * width], og[b, own, :], NT)
    yg[ten] = (yv[:RANK] + yv[RANK:]).astype(BF16)

    pl.semaphore_wait(barrier, nten - 1 + ndp - 1)

    for dev in (right, left, far):
        send(yg.at[ten], yg.at[ten], y_send, y_near, dev)
    send(yg.at[ten], yg.at[ten], y_send, y_sib, sib)

    def send_own(b):
        mine = piece(b, ten)
        send(mine, mine, o_send.at[b], o_left.at[b], right)
        send(mine, mine, o_send.at[b], o_right.at[b], left)
        send(mine, mine, o_send.at[b], o_sib.at[b], sib)

    def pass_near(b):
        from_left, from_right = piece(b, 2 * xl + core), piece(b, 2 * xr + core)
        await_bytes(from_left, o_left.at[b])
        onward = piece(b, 2 * xl + core, 0)
        send(onward, onward, o_send.at[b], o_far.at[b], right)
        send(from_left, from_left, o_send.at[b], o_sib.at[b], sib)
        await_bytes(from_right, o_right.at[b])
        onward = piece(b, 2 * xr + core, 1)
        send(onward, onward, o_send.at[b], o_far.at[b], left)
        send(from_right, from_right, o_send.at[b], o_sib.at[b], sib)

    def pass_far(b):
        from_far = piece(b, 2 * xo + core)
        await_bytes(from_far, o_far.at[b])
        send(from_far, from_far, o_send.at[b], o_sib.at[b], sib)

    def grad_block(b):
        await_bytes(og.at[b, pl.ds(0, rows * NX)], o_sib.at[b])
        mt = min(512, inner)

        @pl.loop(0, inner // mt)
        def _(i):
            r = pl.ds(pl.multiple_of(i * mt, mt), mt)
            gb[r, b * width : (b + 1) * width] = dot(ct[r, :], og[b]).astype(BF16)

    send_own(0)
    send_own(1)

    load_e.wait()
    for n in range(4):
        r = slice(n * inner // 4, (n + 1) * inner // 4)
        v = dot(q2[...], ev[r, :], NT)
        pe[:, r] = v[:RANK] + v[RANK:]
    load_c.wait()
    for t in range(nten):
        ct[:, t * rows : (t + 1) * rows] = cv[t * rows : (t + 1) * rows, :].T

    await_bytes(yg.at[pl.ds(0, 3)], y_near)
    for i in (xl, xr, xo):
        got = yg.at[2 * i + core]
        send(got, got, y_send, y_sib, sib)
    await_bytes(yg.at[pl.ds(0, 4)], y_sib)

    pv = pe[...]
    for t in range(nten):
        pv += dot(yg[t], cv[t * rows : (t + 1) * rows, :])
    pr, pc = RANK // ny, inner // nz
    pv = pv.astype(BF16)
    for k in range(ndp):
        ps[k] = pv[(k % ny) * pr : (k % ny + 1) * pr, (k // ny) * pc : (k // ny + 1) * pc]

    each_replica(lambda to, dev: send(ps.at[to], prx.at[dp], p_send.at[0], p_recv.at[0], dev))

    prx[dp] = ps[dp]
    pass_near(0)
    send_own(2)

    await_bytes(prx.at[pl.ds(0, ndp - 1)], p_recv.at[0])
    total = prx[0].astype(F32)
    for k in range(1, ndp):
        total += prx[k].astype(F32)
    pall[dp] = (total * (1.0 / ndp)).astype(BF16)

    each_replica(lambda to, dev: send(pall.at[dp], pall.at[dp], p_send.at[1], p_recv.at[1], dev))

    pass_near(1)
    send_own(3)
    pass_far(0)
    grad_block(0)

    await_bytes(pall.at[pl.ds(0, ndp - 1)], p_recv.at[1])
    for k in range(ndp):
        pt[(k % ny) * pr : (k % ny + 1) * pr, (k // ny) * pc : (k // ny + 1) * pc] = pall[k]
    gram = dot(pt[...], pt[...], NT)
    gx1[core] = jnp.concatenate([gram[: RANK // 2], gram[RANK // 2 :]], axis=1)
    send(gx1.at[core], gx1.at[core], g_send.at[0], g_recv.at[0], sib)
    pass_far(1)
    pass_near(2)
    ze[...] = dot(pt[...], ev[...])
    await_bytes(gx1.at[0], g_recv.at[0])
    gx2[x] = gx1[0] + gx1[1]
    for dev in (right, left, far):
        send(gx2.at[x], gx2.at[x], g_send.at[1], g_recv.at[1], dev)
    grad_block(1)
    pass_near(3)
    pass_far(2)

    await_bytes(gx2.at[pl.ds(0, NX - 1)], g_recv.at[1])
    gram = gx2[0] + gx2[1] + gx2[2] + gx2[3]
    gram = jnp.concatenate([gram[:, :RANK], gram[:, RANK:]], axis=0)
    on_diag = lax.broadcasted_iota(jnp.int32, (RANK, RANK), 0) == lax.broadcasted_iota(jnp.int32, (RANK, RANK), 1)
    diag = jnp.where(on_diag, gram, 0.0)
    scale = 1.0 / jnp.sqrt(jnp.sum(diag, axis=1, keepdims=True))
    across = 1.0 / jnp.sqrt(jnp.sum(diag, axis=0, keepdims=True))
    gram = jnp.where(on_diag, 1.0, gram * scale * across)
    aug[...] = eliminate(jnp.concatenate([gram, jnp.where(on_diag, across, 0.0)], axis=1), 0, RANK // 2)
    grad_block(2)
    pass_far(3)
    grad_block(3)

    zv = (ze[...] + dot(pt[...], gb[...])).astype(BF16)
    zr, zc = RANK // ny, d // nten
    for k in range(nplane):
        zs[k] = zv[(k % ny) * zr : (k % ny + 1) * zr, (k // ny) * zc : (k // ny + 1) * zc]
    me = ten * ny + y
    each_in_plane(lambda to, dev: send(zs.at[to], z1.at[me], z_send.at[0], z_recv.at[0], dev))
    z1[me] = zs[me]

    load_w.wait()
    out_rows = tokens // 4

    def ctx_chunk(i):
        r = pl.ds(i * out_rows, out_rows)
        for n in range(4):
            c = slice(n * inner // 4, (n + 1) * inner // 4)
            acc = dot(og[0, r, :], wv[c, 0:width], NT)
            for b in range(1, BLOCKS):
                acc += dot(og[b, r, :], wv[c, b * width : (b + 1) * width], NT)
            cs[r, c] = acc.astype(BF16)

    ctx_chunk(0)
    ctx_chunk(1)

    await_bytes(z1.at[pl.ds(0, nplane - 1)], z_recv.at[0])
    total = z1[0].astype(F32)
    for k in range(1, nplane):
        total += z1[k].astype(F32)
    z2[z] = total

    @pl.loop(1, nz)
    def _(i):
        to = wrap(z + i, nz) * ny + y
        send(z2.at[z], z2.at[z], z_send.at[1], z_recv.at[1], {"dp": to})

    a = eliminate(aug[...], RANK // 2, RANK)
    diag = jnp.sum(jnp.where(on_diag, a[:, :RANK], 0.0), axis=1, keepdims=True)
    inv = a[:, RANK:] / jnp.sqrt(diag)
    inv_hi, inv_lo = split(inv)
    lf[...] = jnp.concatenate([inv_hi, inv_lo], axis=1)

    await_bytes(z2.at[pl.ds(0, nz - 1)], z_recv.at[1])
    total = z2[0]
    for k in range(1, nz):
        total += z2[k]
    zall[me] = (total * (1.0 / ndp)).astype(BF16)
    each_in_plane(lambda to, dev: send(zall.at[me], zall.at[me], z_send.at[2], z_recv.at[2], dev))

    f = dot(inv_hi, pt[...]) + dot(inv_lo, pt[...])
    f_hi, f_lo = split(f)
    up_hi, up_lo = split(inv.T)
    pg_hi, pg_lo = split(dot(up_hi, f_hi) + dot(up_hi, f_lo) + dot(up_lo, f_hi))
    ft[...] = jnp.concatenate([pg_hi, pg_lo], axis=0).T

    ctx_chunk(2)
    ctx_chunk(3)

    await_bytes(zall.at[pl.ds(0, nplane - 1)], z_recv.at[2])
    for k in range(nplane):
        zq[(k % ny) * zr : (k % ny + 1) * zr, (k // ny) * zc : (k // ny + 1) * zc] = zall[k]

    await_bytes(yg.at[pl.ds(0, 7)], y_send)
    for b in range(BLOCKS):
        await_bytes(og.at[b, pl.ds(0, 7 * rows)], o_send.at[b])
    await_bytes(prx.at[pl.ds(0, ndp - 1)], p_send.at[0])
    await_bytes(pall.at[pl.ds(0, ndp - 1)], p_send.at[1])
    await_bytes(gx1.at[0], g_send.at[0])
    await_bytes(gx2.at[pl.ds(0, NX - 1)], g_send.at[1])
    await_bytes(z1.at[pl.ds(0, nplane - 1)], z_send.at[0])
    await_bytes(z2.at[pl.ds(0, nz - 1)], z_send.at[1])
    await_bytes(zall.at[pl.ds(0, nplane - 1)], z_send.at[2])


def finish(cs, gb, ev, ft, lf, zq, dctx_hbm, ne_hbm, qf_hbm, ns, qo, store):
    outs = []

    def put(src, dst):
        out = pltpu.make_async_copy(src, dst, store.at[len(outs)])
        out.start()
        outs.append(out)

    put(cs, dctx_hbm)
    zz = jnp.concatenate([zq[...], zq[...]], axis=0)
    step = ns.shape[0] // 4
    for i in range(4):
        r = pl.ds(i * step, step)
        low = dot(ft[r, :], zz)
        ns[r, :] = (gb[r, :].astype(F32) + ev[r, :].astype(F32) - low).astype(BF16)
        put(ns.at[r], ne_hbm.at[0, r])
        if i == 0:
            qo[...] = dot(lf[...], zz)
            put(qo, qf_hbm)
    for out in outs:
        out.wait()


def shards(ny, nz, context, out_grad, out_weight, error, q_init):
    tokens, inner = context.shape
    rows, d = out_grad.shape
    ndp, nplane = ny * nz, 2 * NX * ny
    width = d // BLOCKS
    dma = pltpu.SemaphoreType.DMA
    hbm, in_vmem = pl.BlockSpec(memory_space=pltpu.HBM), pl.BlockSpec(memory_space=pltpu.VMEM)
    pr, pc = RANK // ny, inner // nz
    zr, zc = RANK // ny, d // (2 * NX)
    vm = pltpu.VMEM
    kept = pl.pallas_call(
        functools.partial(kernel, ny, nz),
        out_shape=(
            vm((tokens, inner), BF16),
            vm((inner, d), BF16),
            vm((inner, d), BF16),
            vm((inner, 2 * RANK), BF16),
            vm((RANK, 2 * RANK), BF16),
            vm((RANK, d), BF16),
        ),
        in_specs=[hbm] * 5,
        out_specs=(in_vmem,) * 6,
        scratch_shapes=[
            vm((tokens, inner), BF16),
            vm((inner, tokens), BF16),
            vm((BLOCKS, tokens, width), BF16),
            vm((inner, d), BF16),
            vm((RANK, d), F32),
            vm((2 * RANK, d), BF16),
            vm((2 * NX, RANK, rows), BF16),
            vm((RANK, inner), F32),
            vm((ndp, pr, pc), BF16),
            vm((ndp, pr, pc), BF16),
            vm((ndp, pr, pc), BF16),
            vm((RANK, inner), BF16),
            vm((2, RANK // 2, 2 * RANK), F32),
            vm((NX, RANK // 2, 2 * RANK), F32),
            vm((RANK, 2 * RANK), F32),
            vm((RANK, d), F32),
            vm((nplane, zr, zc), BF16),
            vm((nplane, zr, zc), BF16),
            vm((nz, zr, zc), F32),
            vm((nplane, zr, zc), BF16),
            dma((BLOCKS + 4,)),
            dma, dma, dma,
            dma((BLOCKS,)), dma((BLOCKS,)), dma((BLOCKS,)), dma((BLOCKS,)), dma((BLOCKS,)),
            dma((2,)), dma((2,)), dma((2,)), dma((2,)), dma((3,)), dma((3,)),
        ],
        compiler_params=pltpu.CompilerParams(
            collective_id=0, has_side_effects=True, vmem_limit_bytes=40 * 2**20
        ),
    )(*(pltpu.with_memory_space_constraint(v, pltpu.HBM) for v in (context, out_grad, out_weight, error, q_init.T)))
    dctx, ne, qf = pl.pallas_call(
        finish,
        out_shape=(
            jax.ShapeDtypeStruct((tokens, inner), BF16),
            jax.ShapeDtypeStruct((1, inner, d), BF16),
            jax.ShapeDtypeStruct((RANK, d), F32),
        ),
        in_specs=[in_vmem] * 6,
        out_specs=(hbm,) * 3,
        scratch_shapes=[vm((inner, d), BF16), vm((RANK, d), F32), dma((6,))],
        compiler_params=pltpu.CompilerParams(vmem_limit_bytes=12 * 2**20),
    )(*kept)
    return dctx, ne, qf.T


def solution(mesh):
    ndp = mesh.shape["dp"]
    ny = 4 if ndp % 4 == 0 else 1
    placed = (
        P("dp", "tensor"),
        P(("dp", "tensor"), None),
        P("tensor", None),
        P("dp", "tensor", None),
        P(),
    )
    return jax.shard_map(
        functools.partial(shards, ny, ndp // ny),
        mesh=mesh,
        in_specs=placed,
        out_specs=(P("dp", "tensor"), P("dp", "tensor", None), P()),
        check_vma=False,
    )
```

```python
import functools

import jax
import jax.numpy as jnp
from jax import lax
from jax.experimental import pallas as pl
from jax.experimental.pallas import tpu as pltpu
from jax.sharding import PartitionSpec as P

MESH = pl.DeviceIdType.MESH
F32 = jnp.float32
BF16 = jnp.bfloat16
NX = 4
RANK = 64
FIRST = 16
NT = (((1,), (1,)), ((), ()))
NN = (((1,), (0,)), ((), ()))


def dot(a, b, dims=NN):
    return lax.dot_general(a, b, dims, preferred_element_type=F32)


def split(v):
    hi = v.astype(BF16)
    return hi, (v - hi.astype(F32)).astype(BF16)


def eliminate(a, first, last):
    row_ids = lax.broadcasted_iota(jnp.int32, a.shape, 0)
    for k in range(first, last, 2):
        c0 = jnp.broadcast_to(a[:, k : k + 1], a.shape)
        c1 = jnp.broadcast_to(a[:, k + 1 : k + 2], a.shape)
        r0, r1 = a[k : k + 1, :], a[k + 1 : k + 2, :]
        aa, bb, cc = c0[k : k + 1, :], c0[k + 1 : k + 2, :], c1[k + 1 : k + 2, :]
        inv = 1.0 / (aa * cc - bb * bb)
        w0 = (cc * r0 - bb * r1) * inv
        w1 = (aa * r1 - bb * r0) * inv
        second = r1 - (bb / aa) * r0
        below = a - c0 * w0 - c1 * w1
        a = jnp.where(row_ids > k + 1, below, jnp.where(row_ids == k + 1, second, a))
    return a


def kernel(
    ny, nz,
    ctx_hbm, dy_hbm, w_hbm, e_hbm, q_hbm,
    cs, gb, ev, ft, lf, zq,
    cv, ct, og, wv, wt, acc, qv, q2, yg, pe, ps, prx, pall, pt,
    gx1, gx2, aug, ze, zs, z1, z2, zall,
    load, y_send, y_near, y_sib, o_send, o_left, o_right, o_far, o_sib,
    p_send, p_recv, g_send, g_recv, z_send, z_recv,
):
    dp, ten = lax.axis_index("dp"), lax.axis_index("tensor")
    z, y = dp // ny, dp % ny
    x, core = ten // 2, ten % 2
    ndp, nten = ny * nz, 2 * NX
    nplane = ny * nten
    rows = dy_hbm.shape[0]
    half = rows // 2
    tokens = rows * nten
    inner, d = w_hbm.shape
    xl, xr, xo = lax.rem(x + NX - 1, NX), lax.rem(x + 1, NX), lax.rem(x + 2, NX)
    sib = {"tensor": 2 * x + 1 - core}
    left, right, far = ({"tensor": 2 * i + core} for i in (xl, xr, xo))

    barrier = pltpu.get_barrier_semaphore()

    @pl.loop(1, nten)
    def _(j):
        pl.semaphore_signal(barrier, inc=1, device_id={"tensor": jnp.where(ten + j >= nten, ten + j - nten, ten + j)}, device_id_type=MESH)

    @pl.loop(1, ndp)
    def _(j):
        pl.semaphore_signal(barrier, inc=1, device_id={"dp": jnp.where(dp + j >= ndp, dp + j - ndp, dp + j)}, device_id_type=MESH)

    def piece(owner, part=None):
        if part is None:
            return og.at[pl.ds(pl.multiple_of(owner * rows, rows), rows)]
        return og.at[pl.ds(pl.multiple_of(owner * rows + part * half, half), half)]

    def send(src, dst, s_sem, r_sem, dev):
        pltpu.make_async_remote_copy(
            src_ref=src, dst_ref=dst, send_sem=s_sem, recv_sem=r_sem, device_id=dev, device_id_type=MESH
        ).start()

    def wrap(i, n):
        return jnp.where(i >= n, i - n, i)

    def each_replica(act):
        for j in range(1, ny):
            to_y = wrap(y + j, ny)
            act(z * ny + to_y, {"dp": z * ny + to_y})

        @pl.loop(1, nz)
        def _(i):
            to_z = wrap(z + i, nz)
            for j in range(ny):
                to = to_z * ny + wrap(y + j, ny)
                act(to, {"dp": to})

    def each_in_plane(act):
        for j in range(1, ny):
            to_y = wrap(y + j, ny)
            act(ten * ny + to_y, {"dp": z * ny + to_y})

        @pl.loop(1, nten)
        def _(i):
            to_t = wrap(ten + i, nten)
            for j in range(ny):
                to_y = wrap(y + j, ny)
                act(to_t * ny + to_y, {"dp": z * ny + to_y, "tensor": to_t})

    def await_bytes(ref, sem):
        pltpu.make_async_copy(ref, ref, sem).wait()

    mine = piece(ten)
    load_dy = pltpu.make_async_copy(dy_hbm, mine, load.at[0])
    load_q = pltpu.make_async_copy(q_hbm, qv, load.at[1])
    load_e = pltpu.make_async_copy(e_hbm.at[0], ev, load.at[2])
    load_c = pltpu.make_async_copy(ctx_hbm, cv, load.at[3])
    load_w = pltpu.make_async_copy(w_hbm, wv, load.at[4])
    for c in (load_q, load_dy, load_e, load_c, load_w):
        c.start()

    load_q.wait()
    hi, lo = split(qv[...])
    q2[0:RANK] = hi
    q2[RANK : 2 * RANK] = lo
    load_dy.wait()
    yv = dot(q2[...], mine[...], NT)
    yg[ten] = (yv[:RANK] + yv[RANK:]).astype(BF16)

    pl.semaphore_wait(barrier, nten - 1 + ndp - 1)

    for dev in (right, left, far):
        send(yg.at[ten], yg.at[ten], y_send, y_near, dev)
    send(yg.at[ten], yg.at[ten], y_send, y_sib, sib)

    def pass_on(ref, sem, dev):
        send(ref, ref, o_send, sem, dev)

    for first in (0, 1):
        pass_on(piece(ten, first), o_left.at[first], right)
        pass_on(piece(ten, 1 - first), o_right.at[1 - first], left)
    pass_on(mine, o_sib.at[0], sib)

    def arrive(owner, part, sem):
        await_bytes(piece(owner, part), sem)

    from_left, from_right, from_far = 2 * xl + core, 2 * xr + core, 2 * xo + core

    def rows_of(chip):
        return pl.ds(pl.multiple_of(2 * chip * rows, 2 * rows), 2 * rows)

    mt = inner // 2

    def grad_rows(k, first=False, last=False):
        for i in range(2):
            r = slice(i * mt, (i + 1) * mt)
            v = dot(ct[r, k], og[k, :])
            if not first:
                v += acc[r, :]
            if last:
                gb[r, :] = v.astype(BF16)
            else:
                acc[r, :] = v

    def ctx_rows(k):
        cs[k, :] = dot(og[k, :], wt[...]).astype(BF16)

    load_e.wait()
    v = dot(q2[...], ev[...], NT)
    pe[...] = v[:RANK] + v[RANK:]
    load_c.wait()
    for t in range(nten):
        ct[:, t * rows : (t + 1) * rows] = cv[t * rows : (t + 1) * rows, :].T

    await_bytes(yg.at[pl.ds(0, 3)], y_near)
    for i in (xl, xr, xo):
        got = yg.at[2 * i + core]
        send(got, got, y_send, y_sib, sib)
    load_w.wait()
    wt[...] = wv[...].T
    await_bytes(yg.at[pl.ds(0, 4)], y_sib)

    pv = pe[...] + dot(jnp.concatenate([yg[t] for t in range(nten)], axis=1), cv[...])
    pr, pc = RANK // ny, inner // nz
    pv = pv.astype(BF16)
    for k in range(ndp):
        ps[k] = pv[(k % ny) * pr : (k % ny + 1) * pr, (k // ny) * pc : (k // ny + 1) * pc]

    each_replica(lambda to, dev: send(ps.at[to], prx.at[dp], p_send.at[0], p_recv.at[0], dev))

    prx[dp] = ps[dp]

    await_bytes(mine, o_sib.at[0])
    grad_rows(rows_of(x), first=True)
    arrive(from_left, 0, o_left.at[0])
    pass_on(piece(from_left, 0), o_far.at[0], right)
    arrive(from_right, 1, o_right.at[1])
    pass_on(piece(from_right, 1), o_far.at[1], left)

    await_bytes(prx.at[pl.ds(0, ndp - 1)], p_recv.at[0])
    total = prx[0].astype(F32)
    for k in range(1, ndp):
        total += prx[k].astype(F32)
    pall[dp] = (total * (1.0 / ndp)).astype(BF16)
    each_replica(lambda to, dev: send(pall.at[dp], pall.at[dp], p_send.at[1], p_recv.at[1], dev))

    ctx_rows(rows_of(x))
    arrive(from_left, 1, o_left.at[1])
    pass_on(piece(from_left), o_sib.at[1], sib)
    arrive(from_right, 0, o_right.at[0])
    pass_on(piece(from_right), o_sib.at[2], sib)

    await_bytes(pall.at[pl.ds(0, ndp - 1)], p_recv.at[1])
    for k in range(ndp):
        pt[(k % ny) * pr : (k % ny + 1) * pr, (k // ny) * pc : (k // ny + 1) * pc] = pall[k]
    gram = dot(pt[...], pt[...], NT)
    gx1[core] = jnp.concatenate([gram[: RANK // 2], gram[RANK // 2 :]], axis=1)
    send(gx1.at[core], gx1.at[core], g_send.at[0], g_recv.at[0], sib)
    ze[...] = dot(pt[...], ev[...])
    await_bytes(gx1.at[0], g_recv.at[0])
    gx2[x] = gx1[0] + gx1[1]
    for dev in (right, left, far):
        send(gx2.at[x], gx2.at[x], g_send.at[1], g_recv.at[1], dev)
    await_bytes(piece(from_left), o_sib.at[1])
    grad_rows(rows_of(xl))
    await_bytes(piece(from_right), o_sib.at[2])
    grad_rows(rows_of(xr))

    await_bytes(gx2.at[pl.ds(0, NX - 1)], g_recv.at[1])
    gram = gx2[0] + gx2[1] + gx2[2] + gx2[3]
    gram = jnp.concatenate([gram[:, :RANK], gram[:, RANK:]], axis=0)
    on_diag = lax.broadcasted_iota(jnp.int32, (RANK, RANK), 0) == lax.broadcasted_iota(jnp.int32, (RANK, RANK), 1)
    diag = jnp.where(on_diag, gram, 0.0)
    scale = 1.0 / jnp.sqrt(jnp.sum(diag, axis=1, keepdims=True))
    across = 1.0 / jnp.sqrt(jnp.sum(diag, axis=0, keepdims=True))
    gram = jnp.where(on_diag, 1.0, gram * scale * across)
    aug[...] = eliminate(jnp.concatenate([gram, jnp.where(on_diag, across, 0.0)], axis=1), 0, FIRST)
    for part in (0, 1):
        arrive(from_far, part, o_far.at[part])
        pass_on(piece(from_far, part), o_sib.at[3 + part], sib)
    grad_rows(pl.ds(pl.multiple_of(from_far * rows, rows), rows))
    for part in (0, 1):
        arrive(from_far, part, o_sib.at[3 + part])
    other = 2 * xo + 1 - core
    grad_rows(pl.ds(pl.multiple_of(other * rows, rows), rows), last=True)

    zv = (ze[...] + dot(pt[...], gb[...])).astype(BF16)
    zr, zc = RANK // ny, d // nten
    for k in range(nplane):
        zs[k] = zv[(k % ny) * zr : (k % ny + 1) * zr, (k // ny) * zc : (k // ny + 1) * zc]
    me = ten * ny + y
    each_in_plane(lambda to, dev: send(zs.at[to], z1.at[me], z_send.at[0], z_recv.at[0], dev))
    z1[me] = zs[me]

    ctx_rows(rows_of(xl))
    ctx_rows(rows_of(xr))

    await_bytes(z1.at[pl.ds(0, nplane - 1)], z_recv.at[0])
    total = z1[0].astype(F32)
    for k in range(1, nplane):
        total += z1[k].astype(F32)
    z2[z] = total

    @pl.loop(1, nz)
    def _(i):
        to = wrap(z + i, nz) * ny + y
        send(z2.at[z], z2.at[z], z_send.at[1], z_recv.at[1], {"dp": to})

    a = eliminate(aug[...], FIRST, RANK)
    diag = jnp.sum(jnp.where(on_diag, a[:, :RANK], 0.0), axis=1, keepdims=True)
    inv = a[:, RANK:] / jnp.sqrt(diag)
    inv_hi, inv_lo = split(inv)
    lf[...] = jnp.concatenate([inv_hi, inv_lo], axis=1)

    await_bytes(z2.at[pl.ds(0, nz - 1)], z_recv.at[1])
    total = z2[0]
    for k in range(1, nz):
        total += z2[k]
    zall[me] = (total * (1.0 / ndp)).astype(BF16)
    each_in_plane(lambda to, dev: send(zall.at[me], zall.at[me], z_send.at[2], z_recv.at[2], dev))

    f = dot(inv_hi, pt[...]) + dot(inv_lo, pt[...])
    f_hi, f_lo = split(f)
    up_hi, up_lo = split(inv.T)
    pg_hi, pg_lo = split(dot(up_hi, f_hi) + dot(up_hi, f_lo) + dot(up_lo, f_hi))
    ft[...] = jnp.concatenate([pg_hi, pg_lo], axis=0).T

    ctx_rows(rows_of(xo))

    await_bytes(zall.at[pl.ds(0, nplane - 1)], z_recv.at[2])
    for k in range(nplane):
        zq[(k % ny) * zr : (k % ny + 1) * zr, (k // ny) * zc : (k // ny + 1) * zc] = zall[k]

    await_bytes(yg.at[pl.ds(0, 7)], y_send)
    await_bytes(og.at[pl.ds(0, 7 * rows)], o_send)
    await_bytes(prx.at[pl.ds(0, ndp - 1)], p_send.at[0])
    await_bytes(pall.at[pl.ds(0, ndp - 1)], p_send.at[1])
    await_bytes(gx1.at[0], g_send.at[0])
    await_bytes(gx2.at[pl.ds(0, NX - 1)], g_send.at[1])
    await_bytes(z1.at[pl.ds(0, nplane - 1)], z_send.at[0])
    await_bytes(z2.at[pl.ds(0, nz - 1)], z_send.at[1])
    await_bytes(zall.at[pl.ds(0, nplane - 1)], z_send.at[2])


def finish(cs, gb, ev, ft, lf, zq, dctx_hbm, ne_hbm, qf_hbm, ns, qo, store):
    outs = []

    def put(src, dst):
        out = pltpu.make_async_copy(src, dst, store.at[len(outs)])
        out.start()
        outs.append(out)

    put(cs, dctx_hbm)
    zz = jnp.concatenate([zq[...], zq[...]], axis=0)
    step = ns.shape[0] // 4
    for i in range(4):
        r = pl.ds(i * step, step)
        low = dot(ft[r, :], zz)
        ns[r, :] = (gb[r, :].astype(F32) + ev[r, :].astype(F32) - low).astype(BF16)
        put(ns.at[r], ne_hbm.at[0, r])
        if i == 0:
            qo[...] = dot(lf[...], zz)
            put(qo, qf_hbm)
    for out in outs:
        out.wait()


def shards(ny, nz, context, out_grad, out_weight, error, q_init):
    tokens, inner = context.shape
    rows, d = out_grad.shape
    ndp, nplane = ny * nz, 2 * NX * ny
    dma = pltpu.SemaphoreType.DMA
    hbm, in_vmem = pl.BlockSpec(memory_space=pltpu.HBM), pl.BlockSpec(memory_space=pltpu.VMEM)
    pr, pc = RANK // ny, inner // nz
    zr, zc = RANK // ny, d // (2 * NX)
    vm = pltpu.VMEM
    kept = pl.pallas_call(
        functools.partial(kernel, ny, nz),
        out_shape=(
            vm((tokens, inner), BF16),
            vm((inner, d), BF16),
            vm((inner, d), BF16),
            vm((inner, 2 * RANK), BF16),
            vm((RANK, 2 * RANK), BF16),
            vm((RANK, d), BF16),
        ),
        in_specs=[hbm] * 5,
        out_specs=(in_vmem,) * 6,
        scratch_shapes=[
            vm((tokens, inner), BF16),
            vm((inner, tokens), BF16),
            vm((tokens, d), BF16),
            vm((inner, d), BF16),
            vm((d, inner), BF16),
            vm((inner, d), F32),
            vm((RANK, d), F32),
            vm((2 * RANK, d), BF16),
            vm((2 * NX, RANK, rows), BF16),
            vm((RANK, inner), F32),
            vm((ndp, pr, pc), BF16),
            vm((ndp, pr, pc), BF16),
            vm((ndp, pr, pc), BF16),
            vm((RANK, inner), BF16),
            vm((2, RANK // 2, 2 * RANK), F32),
            vm((NX, RANK // 2, 2 * RANK), F32),
            vm((RANK, 2 * RANK), F32),
            vm((RANK, d), F32),
            vm((nplane, zr, zc), BF16),
            vm((nplane, zr, zc), BF16),
            vm((nz, zr, zc), F32),
            vm((nplane, zr, zc), BF16),
            dma((5,)),
            dma, dma, dma,
            dma, dma((2,)), dma((2,)), dma((2,)), dma((5,)),
            dma((2,)), dma((2,)), dma((2,)), dma((2,)), dma((3,)), dma((3,)),
        ],
        compiler_params=pltpu.CompilerParams(
            collective_id=0, has_side_effects=True, vmem_limit_bytes=40 * 2**20
        ),
    )(*(pltpu.with_memory_space_constraint(v, pltpu.HBM) for v in (context, out_grad, out_weight, error, q_init.T)))
    dctx, ne, qf = pl.pallas_call(
        finish,
        out_shape=(
            jax.ShapeDtypeStruct((tokens, inner), BF16),
            jax.ShapeDtypeStruct((1, inner, d), BF16),
            jax.ShapeDtypeStruct((RANK, d), F32),
        ),
        in_specs=[in_vmem] * 6,
        out_specs=(hbm,) * 3,
        scratch_shapes=[vm((inner, d), BF16), vm((RANK, d), F32), dma((6,))],
        compiler_params=pltpu.CompilerParams(vmem_limit_bytes=12 * 2**20),
    )(*kept)
    return dctx, ne, qf.T


def solution(mesh):
    ndp = mesh.shape["dp"]
    ny = 4 if ndp % 4 == 0 else 1
    placed = (
        P("dp", "tensor"),
        P(("dp", "tensor"), None),
        P("tensor", None),
        P("dp", "tensor", None),
        P(),
    )
    return jax.shard_map(
        functools.partial(shards, ny, ndp // ny),
        mesh=mesh,
        in_specs=placed,
        out_specs=(P("dp", "tensor"), P("dp", "tensor", None), P()),
        check_vma=False,
    )
```

```python
import functools

import jax
import jax.numpy as jnp
from jax import lax
from jax.experimental import pallas as pl
from jax.experimental.pallas import tpu as pltpu
from jax.sharding import PartitionSpec as P

MESH = pl.DeviceIdType.MESH
F32 = jnp.float32
BF16 = jnp.bfloat16
NX = 4
RANK = 64
NT = (((1,), (1,)), ((), ()))
NN = (((1,), (0,)), ((), ()))


def dot(a, b, dims=NN):
    return lax.dot_general(a, b, dims, preferred_element_type=F32)


def split(v):
    hi = v.astype(BF16)
    return hi, (v - hi.astype(F32)).astype(BF16)


def eliminate(a):
    row_ids = lax.broadcasted_iota(jnp.int32, a.shape, 0)
    for k in range(0, a.shape[0], 2):
        c0 = jnp.broadcast_to(a[:, k : k + 1], a.shape)
        c1 = jnp.broadcast_to(a[:, k + 1 : k + 2], a.shape)
        r0, r1 = a[k : k + 1, :], a[k + 1 : k + 2, :]
        aa, bb, cc = c0[k : k + 1, :], c0[k + 1 : k + 2, :], c1[k + 1 : k + 2, :]
        inv = 1.0 / (aa * cc - bb * bb)
        w0 = (cc * r0 - bb * r1) * inv
        w1 = (aa * r1 - bb * r0) * inv
        second = r1 - (bb / aa) * r0
        below = a - c0 * w0 - c1 * w1
        a = jnp.where(row_ids > k + 1, below, jnp.where(row_ids == k + 1, second, a))
    return a


def kernel(
    ny, nz,
    ctx_hbm, dy_hbm, w_hbm, e_hbm, q_hbm,
    cs, gb, ev, ft, lf, zq,
    cv, ct, og, wv, wt, acc, qv, q2, yg, pe, ps, prx, pall, pt,
    gx1, gx2, ze, zs, z1, z2, zall,
    load, y_send, y_near, y_sib, o_send, o_left, o_right, o_far, o_sib,
    p_send, p_recv, g_send, g_recv, z_send, z_recv,
):
    dp, ten = lax.axis_index("dp"), lax.axis_index("tensor")
    z, y = dp // ny, dp % ny
    x, core = ten // 2, ten % 2
    ndp, nten = ny * nz, 2 * NX
    nplane = ny * nten
    rows = dy_hbm.shape[0]
    half = rows // 2
    tokens = rows * nten
    inner, d = w_hbm.shape
    xl, xr, xo = lax.rem(x + NX - 1, NX), lax.rem(x + 1, NX), lax.rem(x + 2, NX)
    sib = {"tensor": 2 * x + 1 - core}
    left, right, far = ({"tensor": 2 * i + core} for i in (xl, xr, xo))

    def piece(owner, part=None):
        if part is None:
            return og.at[pl.ds(pl.multiple_of(owner * rows, rows), rows)]
        return og.at[pl.ds(pl.multiple_of(owner * rows + part * half, half), half)]

    def send(src, dst, s_sem, r_sem, dev):
        pltpu.make_async_remote_copy(
            src_ref=src, dst_ref=dst, send_sem=s_sem, recv_sem=r_sem, device_id=dev, device_id_type=MESH
        ).start()

    def wrap(i, n):
        return jnp.where(i >= n, i - n, i)

    def far_first(n, act):
        act(n // 2)

        @pl.loop(0, n // 2 - 1)
        def _(i):
            act(n // 2 - 1 - i)
            act(n // 2 + 1 + i)

    def each_replica(act):
        def at_z(i):
            to_z = wrap(z + i, nz)
            for j in range(ny):
                to = to_z * ny + wrap(y + j, ny)
                act(to, {"dp": to})

        far_first(nz, at_z)
        for j in range(1, ny):
            to_y = wrap(y + j, ny)
            act(z * ny + to_y, {"dp": z * ny + to_y})

    def each_in_plane(act):
        def at_tensor(i):
            to_t = wrap(ten + i, nten)
            for j in range(ny):
                to_y = wrap(y + j, ny)
                act(to_t * ny + to_y, {"dp": z * ny + to_y, "tensor": to_t})

        far_first(nten, at_tensor)
        for j in range(1, ny):
            to_y = wrap(y + j, ny)
            act(ten * ny + to_y, {"dp": z * ny + to_y})

    def await_bytes(ref, sem):
        pltpu.make_async_copy(ref, ref, sem).wait()

    mine = piece(ten)
    load_dy = pltpu.make_async_copy(dy_hbm, mine, load.at[0])
    load_q = pltpu.make_async_copy(q_hbm, qv, load.at[1])
    load_e = pltpu.make_async_copy(e_hbm.at[0], ev, load.at[2])
    load_c = pltpu.make_async_copy(ctx_hbm, cv, load.at[3])
    load_w = pltpu.make_async_copy(w_hbm, wv, load.at[4])
    load_q.start()
    load_dy.start()

    barrier = pltpu.get_barrier_semaphore()

    @pl.loop(1, nten)
    def _(j):
        pl.semaphore_signal(barrier, inc=1, device_id={"tensor": jnp.where(ten + j >= nten, ten + j - nten, ten + j)}, device_id_type=MESH)

    @pl.loop(1, ndp)
    def _(j):
        pl.semaphore_signal(barrier, inc=1, device_id={"dp": jnp.where(dp + j >= ndp, dp + j - ndp, dp + j)}, device_id_type=MESH)

    for c in (load_e, load_c, load_w):
        c.start()

    load_q.wait()
    hi, lo = split(qv[...])
    q2[0:RANK] = hi
    q2[RANK : 2 * RANK] = lo
    load_dy.wait()
    yv = dot(q2[...], mine[...], NT)
    yg[ten] = (yv[:RANK] + yv[RANK:]).astype(BF16)

    pl.semaphore_wait(barrier, nten - 1 + ndp - 1)

    for dev in (far, right, left):
        send(yg.at[ten], yg.at[ten], y_send, y_near, dev)
    send(yg.at[ten], yg.at[ten], y_send, y_sib, sib)

    def pass_on(ref, sem, dev):
        send(ref, ref, o_send, sem, dev)

    for first in (0, 1):
        pass_on(piece(ten, first), o_left.at[first], right)
        pass_on(piece(ten, 1 - first), o_right.at[1 - first], left)
    pass_on(mine, o_sib.at[0], sib)

    def arrive(owner, part, sem):
        await_bytes(piece(owner, part), sem)

    from_left, from_right, from_far = 2 * xl + core, 2 * xr + core, 2 * xo + core

    def rows_of(chip):
        return pl.ds(pl.multiple_of(2 * chip * rows, 2 * rows), 2 * rows)

    mt = inner // 2

    def grad_rows(k, first=False, last=False):
        for i in range(2):
            r = slice(i * mt, (i + 1) * mt)
            v = dot(ct[r, k], og[k, :])
            if not first:
                v += acc[r, :]
            if last:
                gb[r, :] = v.astype(BF16)
            else:
                acc[r, :] = v

    def ctx_rows(k):
        cs[k, :] = dot(og[k, :], wt[...]).astype(BF16)

    load_e.wait()
    v = dot(q2[...], ev[...], NT)
    pe[...] = v[:RANK] + v[RANK:]
    await_bytes(yg.at[pl.ds(0, 3)], y_near)
    for i in (xl, xr, xo):
        got = yg.at[2 * i + core]
        send(got, got, y_send, y_sib, sib)
    load_c.wait()

    def turn(t):
        ct[:, t * rows : (t + 1) * rows] = cv[t * rows : (t + 1) * rows, :].T

    for t in range(nten // 2):
        turn(t)
    await_bytes(yg.at[pl.ds(0, 4)], y_sib)

    pv = pe[...] + dot(jnp.concatenate([yg[t] for t in range(nten)], axis=1), cv[...])
    pr, pc = RANK // ny, inner // nz
    pv = pv.astype(BF16)
    for k in range(ndp):
        ps[k] = pv[(k % ny) * pr : (k % ny + 1) * pr, (k // ny) * pc : (k // ny + 1) * pc]

    each_replica(lambda to, dev: send(ps.at[to], prx.at[dp], p_send.at[0], p_recv.at[0], dev))

    prx[dp] = ps[dp]

    for t in range(nten // 2, nten):
        turn(t)
    await_bytes(mine, o_sib.at[0])
    grad_rows(rows_of(x), first=True)
    arrive(from_left, 0, o_left.at[0])
    pass_on(piece(from_left, 0), o_far.at[0], right)
    arrive(from_right, 1, o_right.at[1])
    pass_on(piece(from_right, 1), o_far.at[1], left)

    await_bytes(prx.at[pl.ds(0, ndp - 1)], p_recv.at[0])
    total = prx[0].astype(F32)
    for k in range(1, ndp):
        total += prx[k].astype(F32)
    pall[dp] = (total * (1.0 / ndp)).astype(BF16)
    each_replica(lambda to, dev: send(pall.at[dp], pall.at[dp], p_send.at[1], p_recv.at[1], dev))

    load_w.wait()
    wt[...] = wv[...].T
    arrive(from_left, 1, o_left.at[1])
    pass_on(piece(from_left), o_sib.at[1], sib)
    arrive(from_right, 0, o_right.at[0])
    pass_on(piece(from_right), o_sib.at[2], sib)
    ctx_rows(rows_of(x))
    await_bytes(piece(from_left), o_sib.at[1])
    grad_rows(rows_of(xl))
    await_bytes(piece(from_right), o_sib.at[2])
    grad_rows(rows_of(xr))
    for part in (0, 1):
        arrive(from_far, part, o_far.at[part])
        pass_on(piece(from_far, part), o_sib.at[3 + part], sib)
    grad_rows(pl.ds(pl.multiple_of(from_far * rows, rows), rows))

    await_bytes(pall.at[pl.ds(0, ndp - 1)], p_recv.at[1])
    for k in range(ndp):
        pt[(k % ny) * pr : (k % ny + 1) * pr, (k // ny) * pc : (k // ny + 1) * pc] = pall[k]
    gram = dot(pt[...], pt[...], NT)
    gx1[core] = jnp.concatenate([gram[: RANK // 2], gram[RANK // 2 :]], axis=1)
    send(gx1.at[core], gx1.at[core], g_send.at[0], g_recv.at[0], sib)
    ze[...] = dot(pt[...], ev[...])
    for part in (0, 1):
        arrive(from_far, part, o_sib.at[3 + part])
    other = 2 * xo + 1 - core
    grad_rows(pl.ds(pl.multiple_of(other * rows, rows), rows), last=True)

    zv = (ze[...] + dot(pt[...], gb[...])).astype(BF16)
    zr, zc = RANK // ny, d // nten
    for k in range(nplane):
        zs[k] = zv[(k % ny) * zr : (k % ny + 1) * zr, (k // ny) * zc : (k // ny + 1) * zc]
    me = ten * ny + y
    each_in_plane(lambda to, dev: send(zs.at[to], z1.at[me], z_send.at[0], z_recv.at[0], dev))
    z1[me] = zs[me]

    await_bytes(gx1.at[0], g_recv.at[0])
    gx2[x] = gx1[0] + gx1[1]
    for dev in (far, right, left):
        send(gx2.at[x], gx2.at[x], g_send.at[1], g_recv.at[1], dev)
    ctx_rows(rows_of(xl))
    ctx_rows(rows_of(xr))

    await_bytes(z1.at[pl.ds(0, nplane - 1)], z_recv.at[0])
    total = z1[0].astype(F32)
    for k in range(1, nplane):
        total += z1[k].astype(F32)
    z2[z] = total

    far_first(nz, lambda i: send(z2.at[z], z2.at[z], z_send.at[1], z_recv.at[1], {"dp": wrap(z + i, nz) * ny + y}))

    await_bytes(gx2.at[pl.ds(0, NX - 1)], g_recv.at[1])
    gram = gx2[0] + gx2[1] + gx2[2] + gx2[3]
    gram = jnp.concatenate([gram[:, :RANK], gram[:, RANK:]], axis=0)
    on_diag = lax.broadcasted_iota(jnp.int32, (RANK, RANK), 0) == lax.broadcasted_iota(jnp.int32, (RANK, RANK), 1)
    diag = jnp.where(on_diag, gram, 0.0)
    scale = 1.0 / jnp.sqrt(jnp.sum(diag, axis=1, keepdims=True))
    across = 1.0 / jnp.sqrt(jnp.sum(diag, axis=0, keepdims=True))
    gram = jnp.where(on_diag, 1.0, gram * scale * across)
    a = eliminate(jnp.concatenate([gram, jnp.where(on_diag, across, 0.0)], axis=1))
    diag = jnp.sum(jnp.where(on_diag, a[:, :RANK], 0.0), axis=1, keepdims=True)
    inv = a[:, RANK:] / jnp.sqrt(diag)
    inv_hi, inv_lo = split(inv)
    lf[...] = jnp.concatenate([inv_hi, inv_lo], axis=1)

    await_bytes(z2.at[pl.ds(0, nz - 1)], z_recv.at[1])
    total = z2[0]
    for k in range(1, nz):
        total += z2[k]
    zall[me] = (total * (1.0 / ndp)).astype(BF16)
    each_in_plane(lambda to, dev: send(zall.at[me], zall.at[me], z_send.at[2], z_recv.at[2], dev))

    f = dot(inv_hi, pt[...]) + dot(inv_lo, pt[...])
    f_hi, f_lo = split(f)
    up_hi, up_lo = split(inv.T)
    pg_hi, pg_lo = split(dot(up_hi, f_hi) + dot(up_hi, f_lo) + dot(up_lo, f_hi))
    ft[...] = jnp.concatenate([pg_hi, pg_lo], axis=0).T

    ctx_rows(rows_of(xo))

    await_bytes(zall.at[pl.ds(0, nplane - 1)], z_recv.at[2])
    for k in range(nplane):
        zq[(k % ny) * zr : (k % ny + 1) * zr, (k // ny) * zc : (k // ny + 1) * zc] = zall[k]

    await_bytes(yg.at[pl.ds(0, 7)], y_send)
    await_bytes(og.at[pl.ds(0, 7 * rows)], o_send)
    await_bytes(prx.at[pl.ds(0, ndp - 1)], p_send.at[0])
    await_bytes(pall.at[pl.ds(0, ndp - 1)], p_send.at[1])
    await_bytes(gx1.at[0], g_send.at[0])
    await_bytes(gx2.at[pl.ds(0, NX - 1)], g_send.at[1])
    await_bytes(z1.at[pl.ds(0, nplane - 1)], z_send.at[0])
    await_bytes(z2.at[pl.ds(0, nz - 1)], z_send.at[1])
    await_bytes(zall.at[pl.ds(0, nplane - 1)], z_send.at[2])


def finish(cs, gb, ev, ft, lf, zq, dctx_hbm, ne_hbm, qf_hbm, ns, qo, store):
    outs = []

    def put(src, dst):
        out = pltpu.make_async_copy(src, dst, store.at[len(outs)])
        out.start()
        outs.append(out)

    put(cs, dctx_hbm)
    zz = jnp.concatenate([zq[...], zq[...]], axis=0)
    step = ns.shape[0] // 4
    for i in range(4):
        r = pl.ds(i * step, step)
        low = dot(ft[r, :], zz)
        ns[r, :] = (gb[r, :].astype(F32) + ev[r, :].astype(F32) - low).astype(BF16)
        put(ns.at[r], ne_hbm.at[0, r])
        if i == 0:
            qo[...] = dot(lf[...], zz)
            put(qo, qf_hbm)
    for out in outs:
        out.wait()


def shards(ny, nz, context, out_grad, out_weight, error, q_init):
    tokens, inner = context.shape
    rows, d = out_grad.shape
    ndp, nplane = ny * nz, 2 * NX * ny
    dma = pltpu.SemaphoreType.DMA
    hbm, in_vmem = pl.BlockSpec(memory_space=pltpu.HBM), pl.BlockSpec(memory_space=pltpu.VMEM)
    pr, pc = RANK // ny, inner // nz
    zr, zc = RANK // ny, d // (2 * NX)
    vm = pltpu.VMEM
    kept = pl.pallas_call(
        functools.partial(kernel, ny, nz),
        out_shape=(
            vm((tokens, inner), BF16),
            vm((inner, d), BF16),
            vm((inner, d), BF16),
            vm((inner, 2 * RANK), BF16),
            vm((RANK, 2 * RANK), BF16),
            vm((RANK, d), BF16),
        ),
        in_specs=[hbm] * 5,
        out_specs=(in_vmem,) * 6,
        scratch_shapes=[
            vm((tokens, inner), BF16),
            vm((inner, tokens), BF16),
            vm((tokens, d), BF16),
            vm((inner, d), BF16),
            vm((d, inner), BF16),
            vm((inner, d), F32),
            vm((RANK, d), F32),
            vm((2 * RANK, d), BF16),
            vm((2 * NX, RANK, rows), BF16),
            vm((RANK, inner), F32),
            vm((ndp, pr, pc), BF16),
            vm((ndp, pr, pc), BF16),
            vm((ndp, pr, pc), BF16),
            vm((RANK, inner), BF16),
            vm((2, RANK // 2, 2 * RANK), F32),
            vm((NX, RANK // 2, 2 * RANK), F32),
            vm((RANK, d), F32),
            vm((nplane, zr, zc), BF16),
            vm((nplane, zr, zc), BF16),
            vm((nz, zr, zc), F32),
            vm((nplane, zr, zc), BF16),
            dma((5,)),
            dma, dma, dma,
            dma, dma((2,)), dma((2,)), dma((2,)), dma((5,)),
            dma((2,)), dma((2,)), dma((2,)), dma((2,)), dma((3,)), dma((3,)),
        ],
        compiler_params=pltpu.CompilerParams(
            collective_id=0, has_side_effects=True, vmem_limit_bytes=40 * 2**20
        ),
    )(*(pltpu.with_memory_space_constraint(v, pltpu.HBM) for v in (context, out_grad, out_weight, error, q_init.T)))
    dctx, ne, qf = pl.pallas_call(
        finish,
        out_shape=(
            jax.ShapeDtypeStruct((tokens, inner), BF16),
            jax.ShapeDtypeStruct((1, inner, d), BF16),
            jax.ShapeDtypeStruct((RANK, d), F32),
        ),
        in_specs=[in_vmem] * 6,
        out_specs=(hbm,) * 3,
        scratch_shapes=[vm((inner, d), BF16), vm((RANK, d), F32), dma((6,))],
        compiler_params=pltpu.CompilerParams(vmem_limit_bytes=12 * 2**20),
    )(*kept)
    return dctx, ne, qf.T


def solution(mesh):
    ndp = mesh.shape["dp"]
    ny = 4 if ndp % 4 == 0 else 1
    placed = (
        P("dp", "tensor"),
        P(("dp", "tensor"), None),
        P("tensor", None),
        P("dp", "tensor", None),
        P(),
    )
    return jax.shard_map(
        functools.partial(shards, ny, ndp // ny),
        mesh=mesh,
        in_specs=placed,
        out_specs=(P("dp", "tensor"), P("dp", "tensor", None), P()),
        check_vma=False,
    )
```

```python
import functools

import jax
import jax.numpy as jnp
from jax import lax
from jax.experimental import pallas as pl
from jax.experimental.pallas import tpu as pltpu
from jax.sharding import PartitionSpec as P

MESH = pl.DeviceIdType.MESH
F32 = jnp.float32
BF16 = jnp.bfloat16
NX = 4
RANK = 64
NT = (((1,), (1,)), ((), ()))
NN = (((1,), (0,)), ((), ()))


def dot(a, b, dims=NN):
    return lax.dot_general(a, b, dims, preferred_element_type=F32)


def split(v):
    hi = v.astype(BF16)
    return hi, (v - hi.astype(F32)).astype(BF16)


def eliminate(a):
    row_ids = lax.broadcasted_iota(jnp.int32, a.shape, 0)
    for k in range(0, a.shape[0], 2):
        c0 = jnp.broadcast_to(a[:, k : k + 1], a.shape)
        c1 = jnp.broadcast_to(a[:, k + 1 : k + 2], a.shape)
        r0, r1 = a[k : k + 1, :], a[k + 1 : k + 2, :]
        aa, bb, cc = c0[k : k + 1, :], c0[k + 1 : k + 2, :], c1[k + 1 : k + 2, :]
        inv = 1.0 / (aa * cc - bb * bb)
        w0 = (cc * r0 - bb * r1) * inv
        w1 = (aa * r1 - bb * r0) * inv
        second = r1 - (bb / aa) * r0
        below = a - c0 * w0 - c1 * w1
        a = jnp.where(row_ids > k + 1, below, jnp.where(row_ids == k + 1, second, a))
    return a


def kernel(
    ny, nz,
    ctx_hbm, dy_hbm, w_hbm, e_hbm, q_hbm,
    cs, gb, ev, ft, lf, zq,
    cv, ct, og, wv, wt, acc, qv, q2, yg, pe, ps, prx, pall, pt,
    gx1, gx2, zs, z1, z2, zall,
    load, y_send, y_near, y_sib, o_send, o_left, o_right, o_far, o_sib,
    p_send, p_recv, g_send, g_recv, z_send, z_recv,
):
    dp, ten = lax.axis_index("dp"), lax.axis_index("tensor")
    z, y = dp // ny, dp % ny
    x, core = ten // 2, ten % 2
    ndp, nten = ny * nz, 2 * NX
    nplane = ny * nten
    rows = dy_hbm.shape[0]
    half = rows // 2
    tokens = rows * nten
    inner, d = w_hbm.shape
    xl, xr, xo = lax.rem(x + NX - 1, NX), lax.rem(x + 1, NX), lax.rem(x + 2, NX)
    sib = {"tensor": 2 * x + 1 - core}
    left, right, far = ({"tensor": 2 * i + core} for i in (xl, xr, xo))

    OWN, LEFT, RIGHT, FAR = 0, 1, 2, 3

    def piece(slot, part=None, of=core):
        start = 2 * slot * rows + of * rows
        if part is None:
            return og.at[pl.ds(pl.multiple_of(start, rows), rows)]
        return og.at[pl.ds(pl.multiple_of(start + part * half, half), half)]

    def send(src, dst, s_sem, r_sem, dev):
        pltpu.make_async_remote_copy(
            src_ref=src, dst_ref=dst, send_sem=s_sem, recv_sem=r_sem, device_id=dev, device_id_type=MESH
        ).start()

    def wrap(i, n):
        return jnp.where(i >= n, i - n, i)

    def far_first(n, act):
        act(n // 2)

        @pl.loop(0, n // 2 - 1)
        def _(i):
            act(n // 2 - 1 - i)
            act(n // 2 + 1 + i)

    def each_replica(act):
        def at_z(i):
            to_z = wrap(z + i, nz)
            for j in range(ny):
                to = to_z * ny + wrap(y + j, ny)
                act(to, {"dp": to})

        far_first(nz, at_z)
        for j in range(1, ny):
            to_y = wrap(y + j, ny)
            act(z * ny + to_y, {"dp": z * ny + to_y})

    def each_in_plane(act):
        def at_tensor(i):
            to_t = wrap(ten + i, nten)
            for j in range(ny):
                to_y = wrap(y + j, ny)
                act(to_t * ny + to_y, {"dp": z * ny + to_y, "tensor": to_t})

        far_first(nten, at_tensor)
        for j in range(1, ny):
            to_y = wrap(y + j, ny)
            act(ten * ny + to_y, {"dp": z * ny + to_y})

    def await_bytes(ref, sem):
        pltpu.make_async_copy(ref, ref, sem).wait()

    mine = piece(OWN)
    load_dy = pltpu.make_async_copy(dy_hbm, mine, load.at[0])
    load_q = pltpu.make_async_copy(q_hbm, qv, load.at[1])
    load_e = pltpu.make_async_copy(e_hbm.at[0], ev, load.at[2])
    load_c = pltpu.make_async_copy(ctx_hbm, cv, load.at[3])
    load_w = pltpu.make_async_copy(w_hbm, wv, load.at[4])
    load_q.start()
    load_dy.start()

    barrier = pltpu.get_barrier_semaphore()

    @pl.loop(1, nten)
    def _(j):
        pl.semaphore_signal(barrier, inc=1, device_id={"tensor": jnp.where(ten + j >= nten, ten + j - nten, ten + j)}, device_id_type=MESH)

    @pl.loop(1, ndp)
    def _(j):
        pl.semaphore_signal(barrier, inc=1, device_id={"dp": jnp.where(dp + j >= ndp, dp + j - ndp, dp + j)}, device_id_type=MESH)

    for c in (load_e, load_c, load_w):
        c.start()

    load_q.wait()
    hi, lo = split(qv[...])
    q2[0:RANK] = hi
    q2[RANK : 2 * RANK] = lo
    load_dy.wait()
    yv = dot(q2[...], mine[...], NT)
    yg[ten] = (yv[:RANK] + yv[RANK:]).astype(BF16)

    pl.semaphore_wait(barrier, nten - 1 + ndp - 1)

    for dev in (far, right, left):
        send(yg.at[ten], yg.at[ten], y_send, y_near, dev)
    send(yg.at[ten], yg.at[ten], y_send, y_sib, sib)

    def pass_on(src, dst, sem, dev):
        send(src, dst, o_send, sem, dev)

    for first in (0, 1):
        pass_on(piece(OWN, first), piece(LEFT, first), o_left.at[first], right)
        pass_on(piece(OWN, 1 - first), piece(RIGHT, 1 - first), o_right.at[1 - first], left)
    pass_on(mine, mine, o_sib.at[0], sib)

    def hand_over(slot, part, sem):
        ref = piece(slot, part)
        pass_on(ref, ref, sem, sib)

    def slots(first, count=1):
        return slice(2 * first * rows, 2 * (first + count) * rows)

    mt = inner // 2
    halves = [slice(i * mt, (i + 1) * mt) for i in range(2)]

    def ctx_rows(slot, chip):
        to = pl.ds(pl.multiple_of(2 * chip * rows, 2 * rows), 2 * rows)
        cs[to, :] = dot(og[slots(slot), :], wt[...]).astype(BF16)

    load_e.wait()
    v = dot(q2[...], ev[...], NT)
    pe[...] = v[:RANK] + v[RANK:]
    await_bytes(yg.at[pl.ds(0, 3)], y_near)
    for i in (xl, xr, xo):
        got = yg.at[2 * i + core]
        send(got, got, y_send, y_sib, sib)
    load_c.wait()

    def turn(slot, chip):
        for i in range(2):
            src = pl.ds(pl.multiple_of((2 * chip + i) * rows, rows), rows)
            ct[:, (2 * slot + i) * rows : (2 * slot + i + 1) * rows] = cv[src, :].T

    turn(OWN, x)
    turn(LEFT, xl)
    await_bytes(yg.at[pl.ds(0, 4)], y_sib)

    pv = pe[...] + dot(jnp.concatenate([yg[t] for t in range(nten)], axis=1), cv[...])
    pr, pc = RANK // ny, inner // nz
    pv = pv.astype(BF16)
    for k in range(ndp):
        ps[k] = pv[(k % ny) * pr : (k % ny + 1) * pr, (k // ny) * pc : (k // ny + 1) * pc]

    each_replica(lambda to, dev: send(ps.at[to], prx.at[dp], p_send.at[0], p_recv.at[0], dev))

    prx[dp] = ps[dp]

    turn(RIGHT, xr)
    turn(FAR, xo)
    await_bytes(piece(OWN, of=1 - core), o_sib.at[0])
    for r in halves:
        acc[r, :] = dot(ct[r, slots(OWN)], og[slots(OWN), :])
    await_bytes(piece(LEFT, 0), o_left.at[0])
    pass_on(piece(LEFT, 0), piece(FAR, 0), o_far.at[0], right)
    await_bytes(piece(RIGHT, 1), o_right.at[1])
    pass_on(piece(RIGHT, 1), piece(FAR, 1), o_far.at[1], left)
    load_w.wait()
    wt[...] = wv[...].T
    ctx_rows(OWN, x)

    await_bytes(prx.at[pl.ds(0, ndp - 1)], p_recv.at[0])
    total = prx[0].astype(F32)
    for k in range(1, ndp):
        total += prx[k].astype(F32)
    pall[dp] = (total * (1.0 / ndp)).astype(BF16)
    each_replica(lambda to, dev: send(pall.at[dp], pall.at[dp], p_send.at[1], p_recv.at[1], dev))

    await_bytes(piece(LEFT, 1), o_left.at[1])
    hand_over(LEFT, None, o_sib.at[1])
    await_bytes(piece(RIGHT, 0), o_right.at[0])
    hand_over(RIGHT, None, o_sib.at[2])
    await_bytes(piece(LEFT, of=1 - core), o_sib.at[1])
    await_bytes(piece(RIGHT, of=1 - core), o_sib.at[2])
    for r in halves:
        v = acc[r, :] + dot(ct[r, slots(LEFT, 2)], og[slots(LEFT, 2), :])
        acc[r, :] = v
        gb[r, :] = v.astype(BF16)
    ctx_rows(LEFT, xl)
    for part in (0, 1):
        await_bytes(piece(FAR, part), o_far.at[part])
        hand_over(FAR, part, o_sib.at[3 + part])

    await_bytes(pall.at[pl.ds(0, ndp - 1)], p_recv.at[1])
    for k in range(ndp):
        pt[(k % ny) * pr : (k % ny + 1) * pr, (k // ny) * pc : (k // ny + 1) * pc] = pall[k]
    gram = dot(pt[...], pt[...], NT)
    gx1[core] = jnp.concatenate([gram[: RANK // 2], gram[RANK // 2 :]], axis=1)
    send(gx1.at[core], gx1.at[core], g_send.at[0], g_recv.at[0], sib)

    zv = dot(pt[...], ev[...]) + dot(pt[...], gb[...])
    met = dot(pt[...], ct[:, slots(FAR)]).astype(BF16)
    for part in (0, 1):
        await_bytes(piece(FAR, part, 1 - core), o_sib.at[3 + part])
    zv = (zv + dot(met, og[slots(FAR), :])).astype(BF16)
    zr, zc = RANK // ny, d // nten
    for k in range(nplane):
        zs[k] = zv[(k % ny) * zr : (k % ny + 1) * zr, (k // ny) * zc : (k // ny + 1) * zc]
    me = ten * ny + y
    each_in_plane(lambda to, dev: send(zs.at[to], z1.at[me], z_send.at[0], z_recv.at[0], dev))
    z1[me] = zs[me]

    await_bytes(gx1.at[0], g_recv.at[0])
    gx2[x] = gx1[0] + gx1[1]
    for dev in (far, right, left):
        send(gx2.at[x], gx2.at[x], g_send.at[1], g_recv.at[1], dev)
    for r in halves:
        gb[r, :] = (acc[r, :] + dot(ct[r, slots(FAR)], og[slots(FAR), :])).astype(BF16)
    ctx_rows(RIGHT, xr)

    await_bytes(z1.at[pl.ds(0, nplane - 1)], z_recv.at[0])
    total = z1[0].astype(F32)
    for k in range(1, nplane):
        total += z1[k].astype(F32)
    z2[z] = total

    far_first(nz, lambda i: send(z2.at[z], z2.at[z], z_send.at[1], z_recv.at[1], {"dp": wrap(z + i, nz) * ny + y}))

    await_bytes(gx2.at[pl.ds(0, NX - 1)], g_recv.at[1])
    gram = gx2[0] + gx2[1] + gx2[2] + gx2[3]
    gram = jnp.concatenate([gram[:, :RANK], gram[:, RANK:]], axis=0)
    on_diag = lax.broadcasted_iota(jnp.int32, (RANK, RANK), 0) == lax.broadcasted_iota(jnp.int32, (RANK, RANK), 1)
    diag = jnp.where(on_diag, gram, 0.0)
    scale = 1.0 / jnp.sqrt(jnp.sum(diag, axis=1, keepdims=True))
    across = 1.0 / jnp.sqrt(jnp.sum(diag, axis=0, keepdims=True))
    gram = jnp.where(on_diag, 1.0, gram * scale * across)
    a = eliminate(jnp.concatenate([gram, jnp.where(on_diag, across, 0.0)], axis=1))
    diag = jnp.sum(jnp.where(on_diag, a[:, :RANK], 0.0), axis=1, keepdims=True)
    inv = a[:, RANK:] / jnp.sqrt(diag)
    inv_hi, inv_lo = split(inv)
    lf[...] = jnp.concatenate([inv_hi, inv_lo], axis=1)

    await_bytes(z2.at[pl.ds(0, nz - 1)], z_recv.at[1])
    total = z2[0]
    for k in range(1, nz):
        total += z2[k]
    zall[me] = (total * (1.0 / ndp)).astype(BF16)
    each_in_plane(lambda to, dev: send(zall.at[me], zall.at[me], z_send.at[2], z_recv.at[2], dev))

    f = dot(inv_hi, pt[...]) + dot(inv_lo, pt[...])
    f_hi, f_lo = split(f)
    up_hi, up_lo = split(inv.T)
    pg_hi, pg_lo = split(dot(up_hi, f_hi) + dot(up_hi, f_lo) + dot(up_lo, f_hi))
    ft[...] = jnp.concatenate([pg_hi, pg_lo], axis=0).T

    ctx_rows(FAR, xo)

    await_bytes(zall.at[pl.ds(0, nplane - 1)], z_recv.at[2])
    for k in range(nplane):
        zq[(k % ny) * zr : (k % ny + 1) * zr, (k // ny) * zc : (k // ny + 1) * zc] = zall[k]

    await_bytes(yg.at[pl.ds(0, 7)], y_send)
    await_bytes(og.at[pl.ds(0, 7 * rows)], o_send)
    await_bytes(prx.at[pl.ds(0, ndp - 1)], p_send.at[0])
    await_bytes(pall.at[pl.ds(0, ndp - 1)], p_send.at[1])
    await_bytes(gx1.at[0], g_send.at[0])
    await_bytes(gx2.at[pl.ds(0, NX - 1)], g_send.at[1])
    await_bytes(z1.at[pl.ds(0, nplane - 1)], z_send.at[0])
    await_bytes(z2.at[pl.ds(0, nz - 1)], z_send.at[1])
    await_bytes(zall.at[pl.ds(0, nplane - 1)], z_send.at[2])


def finish(cs, gb, ev, ft, lf, zq, dctx_hbm, ne_hbm, qf_hbm, ns, qo, store):
    outs = []

    def put(src, dst):
        out = pltpu.make_async_copy(src, dst, store.at[len(outs)])
        out.start()
        outs.append(out)

    part = cs.shape[0] // 4
    for i in range(4):
        put(cs.at[pl.ds(i * part, part)], dctx_hbm.at[pl.ds(i * part, part)])
    zz = jnp.concatenate([zq[...], zq[...]], axis=0)
    step = ns.shape[0] // 4
    for i in range(4):
        r = pl.ds(i * step, step)
        low = dot(ft[r, :], zz)
        ns[r, :] = (gb[r, :].astype(F32) + ev[r, :].astype(F32) - low).astype(BF16)
        put(ns.at[r], ne_hbm.at[0, r])
        if i == 0:
            qo[...] = dot(lf[...], zz)
            put(qo, qf_hbm)
    for out in outs:
        out.wait()


def shards(ny, nz, context, out_grad, out_weight, error, q_init):
    tokens, inner = context.shape
    rows, d = out_grad.shape
    ndp, nplane = ny * nz, 2 * NX * ny
    dma = pltpu.SemaphoreType.DMA
    hbm, in_vmem = pl.BlockSpec(memory_space=pltpu.HBM), pl.BlockSpec(memory_space=pltpu.VMEM)
    pr, pc = RANK // ny, inner // nz
    zr, zc = RANK // ny, d // (2 * NX)
    vm = pltpu.VMEM
    kept = pl.pallas_call(
        functools.partial(kernel, ny, nz),
        out_shape=(
            vm((tokens, inner), BF16),
            vm((inner, d), BF16),
            vm((inner, d), BF16),
            vm((inner, 2 * RANK), BF16),
            vm((RANK, 2 * RANK), BF16),
            vm((RANK, d), BF16),
        ),
        in_specs=[hbm] * 5,
        out_specs=(in_vmem,) * 6,
        scratch_shapes=[
            vm((tokens, inner), BF16),
            vm((inner, tokens), BF16),
            vm((tokens, d), BF16),
            vm((inner, d), BF16),
            vm((d, inner), BF16),
            vm((inner, d), F32),
            vm((RANK, d), F32),
            vm((2 * RANK, d), BF16),
            vm((2 * NX, RANK, rows), BF16),
            vm((RANK, inner), F32),
            vm((ndp, pr, pc), BF16),
            vm((ndp, pr, pc), BF16),
            vm((ndp, pr, pc), BF16),
            vm((RANK, inner), BF16),
            vm((2, RANK // 2, 2 * RANK), F32),
            vm((NX, RANK // 2, 2 * RANK), F32),
            vm((nplane, zr, zc), BF16),
            vm((nplane, zr, zc), BF16),
            vm((nz, zr, zc), F32),
            vm((nplane, zr, zc), BF16),
            dma((5,)),
            dma, dma, dma,
            dma, dma((2,)), dma((2,)), dma((2,)), dma((5,)),
            dma((2,)), dma((2,)), dma((2,)), dma((2,)), dma((3,)), dma((3,)),
        ],
        compiler_params=pltpu.CompilerParams(
            collective_id=0, has_side_effects=True, vmem_limit_bytes=40 * 2**20
        ),
    )(*(pltpu.with_memory_space_constraint(v, pltpu.HBM) for v in (context, out_grad, out_weight, error, q_init.T)))
    dctx, ne, qf = pl.pallas_call(
        finish,
        out_shape=(
            jax.ShapeDtypeStruct((tokens, inner), BF16),
            jax.ShapeDtypeStruct((1, inner, d), BF16),
            jax.ShapeDtypeStruct((RANK, d), F32),
        ),
        in_specs=[in_vmem] * 6,
        out_specs=(hbm,) * 3,
        scratch_shapes=[vm((inner, d), BF16), vm((RANK, d), F32), dma((9,))],
        compiler_params=pltpu.CompilerParams(vmem_limit_bytes=12 * 2**20),
    )(*kept)
    return dctx, ne, qf.T


def solution(mesh):
    ndp = mesh.shape["dp"]
    ny = 4 if ndp % 4 == 0 else 1
    placed = (
        P("dp", "tensor"),
        P(("dp", "tensor"), None),
        P("tensor", None),
        P("dp", "tensor", None),
        P(),
    )
    return jax.shard_map(
        functools.partial(shards, ny, ndp // ny),
        mesh=mesh,
        in_specs=placed,
        out_specs=(P("dp", "tensor"), P("dp", "tensor", None), P()),
        check_vma=False,
    )
```

```python
import functools

import jax
import jax.numpy as jnp
from jax import lax
from jax.experimental import pallas as pl
from jax.experimental.pallas import tpu as pltpu
from jax.sharding import PartitionSpec as P

MESH = pl.DeviceIdType.MESH
F32 = jnp.float32
BF16 = jnp.bfloat16
NX = 4
RANK = 64
NT = (((1,), (1,)), ((), ()))
NN = (((1,), (0,)), ((), ()))


def dot(a, b, dims=NN):
    return lax.dot_general(a, b, dims, preferred_element_type=F32)


def split(v):
    hi = v.astype(BF16)
    return hi, (v - hi.astype(F32)).astype(BF16)


def eliminate(a, first, last):
    row_ids = lax.broadcasted_iota(jnp.int32, a.shape, 0)
    for k in range(first, last, 2):
        c0 = jnp.broadcast_to(a[:, k : k + 1], a.shape)
        c1 = jnp.broadcast_to(a[:, k + 1 : k + 2], a.shape)
        r0, r1 = a[k : k + 1, :], a[k + 1 : k + 2, :]
        aa, bb, cc = c0[k : k + 1, :], c0[k + 1 : k + 2, :], c1[k + 1 : k + 2, :]
        inv = 1.0 / (aa * cc - bb * bb)
        w0 = (cc * r0 - bb * r1) * inv
        w1 = (aa * r1 - bb * r0) * inv
        second = r1 - (bb / aa) * r0
        below = a - c0 * w0 - c1 * w1
        a = jnp.where(row_ids > k + 1, below, jnp.where(row_ids == k + 1, second, a))
    return a


def kernel(
    ny, nz,
    ctx_hbm, dy_hbm, w_hbm, e_hbm, q_hbm,
    cs, gb, ev, ft, lf, zq,
    cv, ct, og, wv, wt, acc, qv, q2, yg, pe, ps, prx, pex, pall, pt,
    gx1, gx2, zs, z1, z2, zall,
    load, y_send, y_near, y_sib, o_send, o_left, o_right, o_far, o_sib,
    p_send, p_recv, g_send, g_recv, z_send, z_recv,
):
    dp, ten = lax.axis_index("dp"), lax.axis_index("tensor")
    z, y = dp // ny, dp % ny
    x, core = ten // 2, ten % 2
    ndp, nten = ny * nz, 2 * NX
    nplane = ny * nten
    rows = dy_hbm.shape[0]
    half = rows // 2
    tokens = rows * nten
    inner, d = w_hbm.shape
    xl, xr, xo = lax.rem(x + NX - 1, NX), lax.rem(x + 1, NX), lax.rem(x + 2, NX)
    sib = {"tensor": 2 * x + 1 - core}
    left, right, far = ({"tensor": 2 * i + core} for i in (xl, xr, xo))

    OWN, LEFT, RIGHT, FAR = 0, 1, 2, 3

    def piece(slot, part=None, of=core):
        start = 2 * slot * rows + of * rows
        if part is None:
            return og.at[pl.ds(pl.multiple_of(start, rows), rows)]
        return og.at[pl.ds(pl.multiple_of(start + part * half, half), half)]

    def send(src, dst, s_sem, r_sem, dev):
        pltpu.make_async_remote_copy(
            src_ref=src, dst_ref=dst, send_sem=s_sem, recv_sem=r_sem, device_id=dev, device_id_type=MESH
        ).start()

    def wrap(i, n):
        return jnp.where(i >= n, i - n, i)

    def far_first(n, act):
        act(n // 2)

        @pl.loop(0, n // 2 - 1)
        def _(i):
            act(n // 2 - 1 - i)
            act(n // 2 + 1 + i)

    q = nz // 2
    steps = sorted(((d if d <= q // 2 else d - q, d) for d in range(q)), key=lambda p: (-abs(p[0]), p[0]))

    def each_near(sign, act):
        for step, d in steps:
            to_z = lax.rem(z + sign * step + nz, nz)
            for j in range(1 if step == 0 else 0, ny):
                to_y = wrap(y + j, ny)
                act(d, to_z, to_y, {"dp": to_z * ny + to_y})

    def each_in_plane(act):
        def at_tensor(i):
            to_t = wrap(ten + i, nten)
            for j in range(ny):
                to_y = wrap(y + j, ny)
                act(to_t * ny + to_y, {"dp": z * ny + to_y, "tensor": to_t})

        far_first(nten, at_tensor)
        for j in range(1, ny):
            to_y = wrap(y + j, ny)
            act(ten * ny + to_y, {"dp": z * ny + to_y})

    def await_bytes(ref, sem):
        pltpu.make_async_copy(ref, ref, sem).wait()

    mine = piece(OWN)
    load_dy = pltpu.make_async_copy(dy_hbm, mine, load.at[0])
    load_q = pltpu.make_async_copy(q_hbm, qv, load.at[1])
    load_e = pltpu.make_async_copy(e_hbm.at[0], ev, load.at[2])
    load_c = pltpu.make_async_copy(ctx_hbm, cv, load.at[3])
    load_w = pltpu.make_async_copy(w_hbm, wv, load.at[4])
    load_q.start()
    load_dy.start()

    barrier = pltpu.get_barrier_semaphore()

    @pl.loop(1, nten)
    def _(j):
        pl.semaphore_signal(barrier, inc=1, device_id={"tensor": jnp.where(ten + j >= nten, ten + j - nten, ten + j)}, device_id_type=MESH)

    @pl.loop(1, ndp)
    def _(j):
        pl.semaphore_signal(barrier, inc=1, device_id={"dp": jnp.where(dp + j >= ndp, dp + j - ndp, dp + j)}, device_id_type=MESH)

    for c in (load_e, load_c, load_w):
        c.start()

    load_q.wait()
    hi, lo = split(qv[...])
    q2[0:RANK] = hi
    q2[RANK : 2 * RANK] = lo
    load_dy.wait()
    yv = dot(q2[...], mine[...], NT)
    yg[ten] = (yv[:RANK] + yv[RANK:]).astype(BF16)

    pl.semaphore_wait(barrier, nten - 1 + ndp - 1)

    for dev in (far, right, left):
        send(yg.at[ten], yg.at[ten], y_send, y_near, dev)
    send(yg.at[ten], yg.at[ten], y_send, y_sib, sib)

    def pass_on(src, dst, sem, dev):
        send(src, dst, o_send, sem, dev)

    for first in (0, 1):
        pass_on(piece(OWN, first), piece(LEFT, first), o_left.at[first], right)
        pass_on(piece(OWN, 1 - first), piece(RIGHT, 1 - first), o_right.at[1 - first], left)
    pass_on(mine, mine, o_sib.at[0], sib)

    def hand_over(slot, part, sem):
        ref = piece(slot, part)
        pass_on(ref, ref, sem, sib)

    def slots(first, count=1):
        return slice(2 * first * rows, 2 * (first + count) * rows)

    mt = inner // 2
    halves = [slice(i * mt, (i + 1) * mt) for i in range(2)]

    def ctx_rows(slot, chip):
        to = pl.ds(pl.multiple_of(2 * chip * rows, 2 * rows), 2 * rows)
        cs[to, :] = dot(og[slots(slot), :], wt[...]).astype(BF16)

    load_e.wait()
    v = dot(q2[...], ev[...], NT)
    pe[...] = v[:RANK] + v[RANK:]
    await_bytes(yg.at[pl.ds(0, 3)], y_near)
    for i in (xl, xr, xo):
        got = yg.at[2 * i + core]
        send(got, got, y_send, y_sib, sib)
    load_c.wait()

    def turn(slot, chip):
        for i in range(2):
            src = pl.ds(pl.multiple_of((2 * chip + i) * rows, rows), rows)
            ct[:, (2 * slot + i) * rows : (2 * slot + i + 1) * rows] = cv[src, :].T

    turn(OWN, x)
    turn(LEFT, xl)
    await_bytes(yg.at[pl.ds(0, 4)], y_sib)

    pv = pe[...] + dot(jnp.concatenate([yg[t] for t in range(nten)], axis=1), cv[...])
    pr, pc = RANK // ny, inner // q
    pv = pv.astype(BF16)
    for k in range(ny * q):
        ps[k] = pv[(k % ny) * pr : (k % ny + 1) * pr, (k // ny) * pc : (k // ny + 1) * pc]

    def to_owner(d, to_z, to_y, dev):
        send(ps.at[lax.rem(to_z, q) * ny + to_y], prx.at[d * ny + y], p_send.at[0], p_recv.at[0], dev)

    each_near(1, to_owner)
    own_piece = lax.rem(z, q) * ny + y
    prx[y] = ps[own_piece]

    turn(RIGHT, xr)
    turn(FAR, xo)
    await_bytes(piece(OWN, of=1 - core), o_sib.at[0])
    for r in halves:
        acc[r, :] = dot(ct[r, slots(OWN)], og[slots(OWN), :])
    await_bytes(piece(LEFT, 0), o_left.at[0])
    pass_on(piece(LEFT, 0), piece(FAR, 0), o_far.at[0], right)
    await_bytes(piece(RIGHT, 1), o_right.at[1])
    pass_on(piece(RIGHT, 1), piece(FAR, 1), o_far.at[1], left)
    load_w.wait()
    wt[...] = wv[...].T

    await_bytes(prx.at[pl.ds(0, ny * q - 1)], p_recv.at[0])
    total = prx[0].astype(F32)
    for k in range(1, ny * q):
        total += prx[k].astype(F32)
    side = z // q
    pex[side] = total.astype(BF16)
    send(pex.at[side], pex.at[side], p_send.at[1], p_recv.at[1], {"dp": lax.rem(z + q, nz) * ny + y})
    ctx_rows(OWN, x)
    await_bytes(pex.at[0], p_recv.at[1])
    pall[own_piece] = ((pex[0].astype(F32) + pex[1].astype(F32)) * (1.0 / ndp)).astype(BF16)
    each_near(
        -1, lambda d, to_z, to_y, dev: send(pall.at[own_piece], pall.at[own_piece], p_send.at[2], p_recv.at[2], dev)
    )

    await_bytes(piece(LEFT, 1), o_left.at[1])
    hand_over(LEFT, None, o_sib.at[1])
    await_bytes(piece(RIGHT, 0), o_right.at[0])
    hand_over(RIGHT, None, o_sib.at[2])
    await_bytes(piece(LEFT, of=1 - core), o_sib.at[1])
    await_bytes(piece(RIGHT, of=1 - core), o_sib.at[2])
    for r in halves:
        v = acc[r, :] + dot(ct[r, slots(LEFT, 2)], og[slots(LEFT, 2), :])
        acc[r, :] = v
        gb[r, :] = v.astype(BF16)
    ctx_rows(LEFT, xl)
    for part in (0, 1):
        await_bytes(piece(FAR, part), o_far.at[part])
        hand_over(FAR, part, o_sib.at[3 + part])

    await_bytes(pall.at[pl.ds(0, ny * q - 1)], p_recv.at[2])
    for k in range(ny * q):
        pt[(k % ny) * pr : (k % ny + 1) * pr, (k // ny) * pc : (k // ny + 1) * pc] = pall[k]
    gram = dot(pt[...], pt[...], NT)
    gx1[core] = jnp.concatenate([gram[: RANK // 2], gram[RANK // 2 :]], axis=1)
    send(gx1.at[core], gx1.at[core], g_send.at[0], g_recv.at[0], sib)

    zv = dot(pt[...], ev[...]) + dot(pt[...], gb[...])
    met = dot(pt[...], ct[:, slots(FAR)]).astype(BF16)
    for part in (0, 1):
        await_bytes(piece(FAR, part, 1 - core), o_sib.at[3 + part])
    zv = (zv + dot(met, og[slots(FAR), :])).astype(BF16)
    zr, zc = RANK // ny, d // nten
    for k in range(nplane):
        zs[k] = zv[(k % ny) * zr : (k % ny + 1) * zr, (k // ny) * zc : (k // ny + 1) * zc]
    me = ten * ny + y
    each_in_plane(lambda to, dev: send(zs.at[to], z1.at[me], z_send.at[0], z_recv.at[0], dev))
    z1[me] = zs[me]

    await_bytes(gx1.at[0], g_recv.at[0])
    gx2[x] = gx1[0] + gx1[1]
    for dev in (far, right, left):
        send(gx2.at[x], gx2.at[x], g_send.at[1], g_recv.at[1], dev)
    for r in halves:
        gb[r, :] = (acc[r, :] + dot(ct[r, slots(FAR)], og[slots(FAR), :])).astype(BF16)
    ctx_rows(RIGHT, xr)

    await_bytes(gx2.at[pl.ds(0, NX - 1)], g_recv.at[1])
    gram = gx2[0] + gx2[1] + gx2[2] + gx2[3]
    gram = jnp.concatenate([gram[:, :RANK], gram[:, RANK:]], axis=0)
    on_diag = lax.broadcasted_iota(jnp.int32, (RANK, RANK), 0) == lax.broadcasted_iota(jnp.int32, (RANK, RANK), 1)
    diag = jnp.where(on_diag, gram, 0.0)
    scale = 1.0 / jnp.sqrt(jnp.sum(diag, axis=1, keepdims=True))
    across = 1.0 / jnp.sqrt(jnp.sum(diag, axis=0, keepdims=True))
    gram = jnp.where(on_diag, 1.0, gram * scale * across)
    a = eliminate(jnp.concatenate([gram, jnp.where(on_diag, across, 0.0)], axis=1), 0, RANK // 2)

    await_bytes(z1.at[pl.ds(0, nplane - 1)], z_recv.at[0])
    total = z1[0].astype(F32)
    for k in range(1, nplane):
        total += z1[k].astype(F32)
    z2[z] = total.astype(BF16)

    far_first(nz, lambda i: send(z2.at[z], z2.at[z], z_send.at[1], z_recv.at[1], {"dp": wrap(z + i, nz) * ny + y}))

    a = eliminate(a, RANK // 2, RANK)
    diag = jnp.sum(jnp.where(on_diag, a[:, :RANK], 0.0), axis=1, keepdims=True)
    inv = a[:, RANK:] / jnp.sqrt(diag)
    inv_hi, inv_lo = split(inv)
    lf[...] = jnp.concatenate([inv_hi, inv_lo], axis=1)

    await_bytes(z2.at[pl.ds(0, nz - 1)], z_recv.at[1])
    total = z2[0].astype(F32)
    for k in range(1, nz):
        total += z2[k].astype(F32)
    zall[me] = (total * (1.0 / ndp)).astype(BF16)
    each_in_plane(lambda to, dev: send(zall.at[me], zall.at[me], z_send.at[2], z_recv.at[2], dev))

    f = dot(inv_hi, pt[...]) + dot(inv_lo, pt[...])
    f_hi, f_lo = split(f)
    up_hi, up_lo = split(inv.T)
    pg_hi, pg_lo = split(dot(up_hi, f_hi) + dot(up_hi, f_lo) + dot(up_lo, f_hi))
    ft[...] = jnp.concatenate([pg_hi, pg_lo], axis=0).T

    ctx_rows(FAR, xo)

    await_bytes(zall.at[pl.ds(0, nplane - 1)], z_recv.at[2])
    for k in range(nplane):
        zq[(k % ny) * zr : (k % ny + 1) * zr, (k // ny) * zc : (k // ny + 1) * zc] = zall[k]

    await_bytes(yg.at[pl.ds(0, 7)], y_send)
    await_bytes(og.at[pl.ds(0, 7 * rows)], o_send)
    await_bytes(prx.at[pl.ds(0, ny * q - 1)], p_send.at[0])
    await_bytes(pex.at[0], p_send.at[1])
    await_bytes(pall.at[pl.ds(0, ny * q - 1)], p_send.at[2])
    await_bytes(gx1.at[0], g_send.at[0])
    await_bytes(gx2.at[pl.ds(0, NX - 1)], g_send.at[1])
    await_bytes(z1.at[pl.ds(0, nplane - 1)], z_send.at[0])
    await_bytes(z2.at[pl.ds(0, nz - 1)], z_send.at[1])
    await_bytes(zall.at[pl.ds(0, nplane - 1)], z_send.at[2])


def finish(cs, gb, ev, ft, lf, zq, dctx_hbm, ne_hbm, qf_hbm, ns, qo, store):
    outs = []

    def put(src, dst):
        out = pltpu.make_async_copy(src, dst, store.at[len(outs)])
        out.start()
        outs.append(out)

    part = cs.shape[0] // 4
    for i in range(4):
        put(cs.at[pl.ds(i * part, part)], dctx_hbm.at[pl.ds(i * part, part)])
    zz = jnp.concatenate([zq[...], zq[...]], axis=0)
    step = ns.shape[0] // 4
    for i in range(4):
        r = pl.ds(i * step, step)
        low = dot(ft[r, :], zz)
        ns[r, :] = (gb[r, :].astype(F32) + ev[r, :].astype(F32) - low).astype(BF16)
        put(ns.at[r], ne_hbm.at[0, r])
        if i == 0:
            qo[...] = dot(lf[...], zz)
            put(qo, qf_hbm)
    for out in outs:
        out.wait()


def shards(ny, nz, context, out_grad, out_weight, error, q_init):
    tokens, inner = context.shape
    rows, d = out_grad.shape
    nplane = 2 * NX * ny
    dma = pltpu.SemaphoreType.DMA
    hbm, in_vmem = pl.BlockSpec(memory_space=pltpu.HBM), pl.BlockSpec(memory_space=pltpu.VMEM)
    q = nz // 2
    pr, pc = RANK // ny, inner // q
    zr, zc = RANK // ny, d // (2 * NX)
    vm = pltpu.VMEM
    kept = pl.pallas_call(
        functools.partial(kernel, ny, nz),
        out_shape=(
            vm((tokens, inner), BF16),
            vm((inner, d), BF16),
            vm((inner, d), BF16),
            vm((inner, 2 * RANK), BF16),
            vm((RANK, 2 * RANK), BF16),
            vm((RANK, d), BF16),
        ),
        in_specs=[hbm] * 5,
        out_specs=(in_vmem,) * 6,
        scratch_shapes=[
            vm((tokens, inner), BF16),
            vm((inner, tokens), BF16),
            vm((tokens, d), BF16),
            vm((inner, d), BF16),
            vm((d, inner), BF16),
            vm((inner, d), F32),
            vm((RANK, d), F32),
            vm((2 * RANK, d), BF16),
            vm((2 * NX, RANK, rows), BF16),
            vm((RANK, inner), F32),
            vm((ny * q, pr, pc), BF16),
            vm((ny * q, pr, pc), BF16),
            vm((2, pr, pc), BF16),
            vm((ny * q, pr, pc), BF16),
            vm((RANK, inner), BF16),
            vm((2, RANK // 2, 2 * RANK), F32),
            vm((NX, RANK // 2, 2 * RANK), F32),
            vm((nplane, zr, zc), BF16),
            vm((nplane, zr, zc), BF16),
            vm((nz, zr, zc), BF16),
            vm((nplane, zr, zc), BF16),
            dma((5,)),
            dma, dma, dma,
            dma, dma((2,)), dma((2,)), dma((2,)), dma((5,)),
            dma((3,)), dma((3,)), dma((2,)), dma((2,)), dma((3,)), dma((3,)),
        ],
        compiler_params=pltpu.CompilerParams(
            collective_id=0, has_side_effects=True, vmem_limit_bytes=40 * 2**20
        ),
    )(*(pltpu.with_memory_space_constraint(v, pltpu.HBM) for v in (context, out_grad, out_weight, error, q_init.T)))
    dctx, ne, qf = pl.pallas_call(
        finish,
        out_shape=(
            jax.ShapeDtypeStruct((tokens, inner), BF16),
            jax.ShapeDtypeStruct((1, inner, d), BF16),
            jax.ShapeDtypeStruct((RANK, d), F32),
        ),
        in_specs=[in_vmem] * 6,
        out_specs=(hbm,) * 3,
        scratch_shapes=[vm((inner, d), BF16), vm((RANK, d), F32), dma((9,))],
        compiler_params=pltpu.CompilerParams(vmem_limit_bytes=12 * 2**20),
    )(*kept)
    return dctx, ne, qf.T


def solution(mesh):
    ndp = mesh.shape["dp"]
    ny = 4 if ndp % 4 == 0 else 1
    placed = (
        P("dp", "tensor"),
        P(("dp", "tensor"), None),
        P("tensor", None),
        P("dp", "tensor", None),
        P(),
    )
    return jax.shard_map(
        functools.partial(shards, ny, ndp // ny),
        mesh=mesh,
        in_specs=placed,
        out_specs=(P("dp", "tensor"), P("dp", "tensor", None), P()),
        check_vma=False,
    )
```

```python
import functools

import jax
import jax.numpy as jnp
from jax import lax
from jax.experimental import pallas as pl
from jax.experimental.pallas import tpu as pltpu
from jax.sharding import PartitionSpec as P

MESH = pl.DeviceIdType.MESH
F32 = jnp.float32
BF16 = jnp.bfloat16
NX = 4
RANK = 64
NT = (((1,), (1,)), ((), ()))
NN = (((1,), (0,)), ((), ()))


def dot(a, b, dims=NN):
    return lax.dot_general(a, b, dims, preferred_element_type=F32)


def split(v):
    hi = v.astype(BF16)
    return hi, (v - hi.astype(F32)).astype(BF16)


def eliminate(a):
    row_ids = lax.broadcasted_iota(jnp.int32, a.shape, 0)
    for k in range(0, a.shape[0], 2):
        c0 = jnp.broadcast_to(a[:, k : k + 1], a.shape)
        c1 = jnp.broadcast_to(a[:, k + 1 : k + 2], a.shape)
        r0, r1 = a[k : k + 1, :], a[k + 1 : k + 2, :]
        aa, bb, cc = c0[k : k + 1, :], c0[k + 1 : k + 2, :], c1[k + 1 : k + 2, :]
        inv = 1.0 / (aa * cc - bb * bb)
        w0 = (cc * r0 - bb * r1) * inv
        w1 = (aa * r1 - bb * r0) * inv
        second = r1 - (bb / aa) * r0
        below = a - c0 * w0 - c1 * w1
        a = jnp.where(row_ids > k + 1, below, jnp.where(row_ids == k + 1, second, a))
    return a


def kernel(
    ny, nz,
    ctx_hbm, dy_hbm, w_hbm, e_hbm, q_hbm,
    cs, gb, ev, ft, lf, zq,
    cv, ct, og, wv, wt, acc, qv, q2, yg, pe, ps, prx, pall, pt,
    gx1, gx2, zs, z1, z2, zall,
    load, y_send, y_near, y_sib, o_send, o_left, o_right, o_far, o_sib,
    p_send, p_recv, g_send, g_recv, z_send, z_recv,
):
    dp, ten = lax.axis_index("dp"), lax.axis_index("tensor")
    z, y = dp // ny, dp % ny
    x, core = ten // 2, ten % 2
    ndp, nten = ny * nz, 2 * NX
    nplane = ny * nten
    rows = dy_hbm.shape[0]
    half = rows // 2
    tokens = rows * nten
    inner, d = w_hbm.shape
    xl, xr, xo = lax.rem(x + NX - 1, NX), lax.rem(x + 1, NX), lax.rem(x + 2, NX)
    sib = {"tensor": 2 * x + 1 - core}
    left, right, far = ({"tensor": 2 * i + core} for i in (xl, xr, xo))

    OWN, LEFT, RIGHT, FAR = 0, 1, 2, 3

    def piece(slot, part=None, of=core):
        start = 2 * slot * rows + of * rows
        if part is None:
            return og.at[pl.ds(pl.multiple_of(start, rows), rows)]
        return og.at[pl.ds(pl.multiple_of(start + part * half, half), half)]

    def send(src, dst, s_sem, r_sem, dev):
        pltpu.make_async_remote_copy(
            src_ref=src, dst_ref=dst, send_sem=s_sem, recv_sem=r_sem, device_id=dev, device_id_type=MESH
        ).start()

    def wrap(i, n):
        return jnp.where(i >= n, i - n, i)

    def far_first(n, act):
        act(n // 2)

        @pl.loop(0, n // 2 - 1)
        def _(i):
            act(n // 2 - 1 - i)
            act(n // 2 + 1 + i)

    def each_replica(act):
        def at_z(i):
            to_z = wrap(z + i, nz)
            for j in range(ny):
                to = to_z * ny + wrap(y + j, ny)
                act(to, {"dp": to})

        far_first(nz, at_z)
        for j in range(1, ny):
            to_y = wrap(y + j, ny)
            act(z * ny + to_y, {"dp": z * ny + to_y})

    def each_in_plane(act):
        def at_tensor(i):
            to_t = wrap(ten + i, nten)
            for j in range(ny):
                to_y = wrap(y + j, ny)
                act(to_t * ny + to_y, {"dp": z * ny + to_y, "tensor": to_t})

        far_first(nten, at_tensor)
        for j in range(1, ny):
            to_y = wrap(y + j, ny)
            act(ten * ny + to_y, {"dp": z * ny + to_y})

    def await_bytes(ref, sem):
        pltpu.make_async_copy(ref, ref, sem).wait()

    mine = piece(OWN)
    load_dy = pltpu.make_async_copy(dy_hbm, mine, load.at[0])
    load_q = pltpu.make_async_copy(q_hbm, qv, load.at[1])
    load_e = pltpu.make_async_copy(e_hbm.at[0], ev, load.at[2])
    load_c = pltpu.make_async_copy(ctx_hbm, cv, load.at[3])
    load_w = pltpu.make_async_copy(w_hbm, wv, load.at[4])
    load_q.start()
    load_dy.start()

    barrier = pltpu.get_barrier_semaphore()

    @pl.loop(1, nten)
    def _(j):
        pl.semaphore_signal(barrier, inc=1, device_id={"tensor": jnp.where(ten + j >= nten, ten + j - nten, ten + j)}, device_id_type=MESH)

    @pl.loop(1, ndp)
    def _(j):
        pl.semaphore_signal(barrier, inc=1, device_id={"dp": jnp.where(dp + j >= ndp, dp + j - ndp, dp + j)}, device_id_type=MESH)

    for c in (load_e, load_c, load_w):
        c.start()

    load_q.wait()
    hi, lo = split(qv[...])
    q2[0:RANK] = hi
    q2[RANK : 2 * RANK] = lo
    load_dy.wait()
    yv = dot(q2[...], mine[...], NT)
    yg[ten] = (yv[:RANK] + yv[RANK:]).astype(BF16)

    pl.semaphore_wait(barrier, nten - 1 + ndp - 1)

    for dev in (far, right, left):
        send(yg.at[ten], yg.at[ten], y_send, y_near, dev)
    send(yg.at[ten], yg.at[ten], y_send, y_sib, sib)

    def pass_on(src, dst, sem, dev):
        send(src, dst, o_send, sem, dev)

    for first in (0, 1):
        pass_on(piece(OWN, first), piece(LEFT, first), o_left.at[first], right)
        pass_on(piece(OWN, 1 - first), piece(RIGHT, 1 - first), o_right.at[1 - first], left)
    pass_on(mine, mine, o_sib.at[0], sib)

    def hand_over(slot, part, sem):
        ref = piece(slot, part)
        pass_on(ref, ref, sem, sib)

    def slots(first, count=1):
        return slice(2 * first * rows, 2 * (first + count) * rows)

    mt = inner // 2
    halves = [slice(i * mt, (i + 1) * mt) for i in range(2)]

    def ctx_rows(slot, chip):
        to = pl.ds(pl.multiple_of(2 * chip * rows, 2 * rows), 2 * rows)
        cs[to, :] = dot(og[slots(slot), :], wt[...]).astype(BF16)

    load_e.wait()
    v = dot(q2[...], ev[...], NT)
    pe[...] = v[:RANK] + v[RANK:]
    await_bytes(yg.at[pl.ds(0, 3)], y_near)
    for i in (xl, xr, xo):
        got = yg.at[2 * i + core]
        send(got, got, y_send, y_sib, sib)
    load_c.wait()

    def turn(slot, chip):
        for i in range(2):
            src = pl.ds(pl.multiple_of((2 * chip + i) * rows, rows), rows)
            ct[:, (2 * slot + i) * rows : (2 * slot + i + 1) * rows] = cv[src, :].T

    turn(OWN, x)
    turn(LEFT, xl)
    await_bytes(yg.at[pl.ds(0, 4)], y_sib)

    pv = pe[...] + dot(jnp.concatenate([yg[t] for t in range(nten)], axis=1), cv[...])
    pr, pc = RANK // ny, inner // nz
    pv = pv.astype(BF16)
    for k in range(ndp):
        ps[k] = pv[(k % ny) * pr : (k % ny + 1) * pr, (k // ny) * pc : (k // ny + 1) * pc]

    each_replica(lambda to, dev: send(ps.at[to], prx.at[dp], p_send.at[0], p_recv.at[0], dev))

    prx[dp] = ps[dp]

    turn(RIGHT, xr)
    turn(FAR, xo)
    await_bytes(piece(LEFT, 0), o_left.at[0])
    pass_on(piece(LEFT, 0), piece(FAR, 0), o_far.at[0], right)
    await_bytes(piece(RIGHT, 1), o_right.at[1])
    pass_on(piece(RIGHT, 1), piece(FAR, 1), o_far.at[1], left)
    load_w.wait()
    wt[...] = wv[...].T
    await_bytes(piece(OWN, of=1 - core), o_sib.at[0])
    ctx_rows(OWN, x)

    await_bytes(prx.at[pl.ds(0, ndp - 1)], p_recv.at[0])
    total = prx[0].astype(F32)
    for k in range(1, ndp):
        total += prx[k].astype(F32)
    pall[dp] = (total * (1.0 / ndp)).astype(BF16)
    each_replica(lambda to, dev: send(pall.at[dp], pall.at[dp], p_send.at[1], p_recv.at[1], dev))

    await_bytes(piece(LEFT, 1), o_left.at[1])
    hand_over(LEFT, None, o_sib.at[1])
    await_bytes(piece(RIGHT, 0), o_right.at[0])
    hand_over(RIGHT, None, o_sib.at[2])
    await_bytes(piece(LEFT, of=1 - core), o_sib.at[1])
    await_bytes(piece(RIGHT, of=1 - core), o_sib.at[2])
    for r in halves:
        v = dot(ct[r, slots(OWN, 3)], og[slots(OWN, 3), :])
        acc[r, :] = v
        gb[r, :] = v.astype(BF16)
    ctx_rows(LEFT, xl)
    for part in (0, 1):
        await_bytes(piece(FAR, part), o_far.at[part])
        hand_over(FAR, part, o_sib.at[3 + part])

    await_bytes(pall.at[pl.ds(0, ndp - 1)], p_recv.at[1])
    for k in range(ndp):
        pt[(k % ny) * pr : (k % ny + 1) * pr, (k // ny) * pc : (k // ny + 1) * pc] = pall[k]
    zv = dot(pt[...], ev[...]) + dot(pt[...], gb[...])
    met = dot(pt[...], ct[:, slots(FAR)]).astype(BF16)
    for part in (0, 1):
        await_bytes(piece(FAR, part, 1 - core), o_sib.at[3 + part])
    zv = (zv + dot(met, og[slots(FAR), :])).astype(BF16)
    zr, zc = RANK // ny, d // nten
    for k in range(nplane):
        zs[k] = zv[(k % ny) * zr : (k % ny + 1) * zr, (k // ny) * zc : (k // ny + 1) * zc]
    me = ten * ny + y
    each_in_plane(lambda to, dev: send(zs.at[to], z1.at[me], z_send.at[0], z_recv.at[0], dev))
    z1[me] = zs[me]

    gram = dot(pt[...], pt[...], NT)
    gx1[core] = jnp.concatenate([gram[: RANK // 2], gram[RANK // 2 :]], axis=1)
    send(gx1.at[core], gx1.at[core], g_send.at[0], g_recv.at[0], sib)

    def last_rows(r):
        gb[r, :] = (acc[r, :] + dot(ct[r, slots(FAR)], og[slots(FAR), :])).astype(BF16)

    last_rows(halves[0])
    await_bytes(gx1.at[0], g_recv.at[0])
    gx2[x] = gx1[0] + gx1[1]
    for dev in (far, right, left):
        send(gx2.at[x], gx2.at[x], g_send.at[1], g_recv.at[1], dev)
    last_rows(halves[1])

    await_bytes(z1.at[pl.ds(0, nplane - 1)], z_recv.at[0])
    total = z1[0].astype(F32)
    for k in range(1, nplane):
        total += z1[k].astype(F32)
    z2[z] = total.astype(BF16)

    far_first(nz, lambda i: send(z2.at[z], z2.at[z], z_send.at[1], z_recv.at[1], {"dp": wrap(z + i, nz) * ny + y}))

    await_bytes(gx2.at[pl.ds(0, NX - 1)], g_recv.at[1])
    gram = gx2[0] + gx2[1] + gx2[2] + gx2[3]
    gram = jnp.concatenate([gram[:, :RANK], gram[:, RANK:]], axis=0)
    on_diag = lax.broadcasted_iota(jnp.int32, (RANK, RANK), 0) == lax.broadcasted_iota(jnp.int32, (RANK, RANK), 1)
    diag = jnp.where(on_diag, gram, 0.0)
    scale = 1.0 / jnp.sqrt(jnp.sum(diag, axis=1, keepdims=True))
    across = 1.0 / jnp.sqrt(jnp.sum(diag, axis=0, keepdims=True))
    gram = jnp.where(on_diag, 1.0, gram * scale * across)
    a = eliminate(jnp.concatenate([gram, jnp.where(on_diag, across, 0.0)], axis=1))
    diag = jnp.sum(jnp.where(on_diag, a[:, :RANK], 0.0), axis=1, keepdims=True)
    inv = a[:, RANK:] / jnp.sqrt(diag)
    ctx_rows(RIGHT, xr)
    inv_hi, inv_lo = split(inv)
    lf[...] = jnp.concatenate([inv_hi, inv_lo], axis=1)

    await_bytes(z2.at[pl.ds(0, nz - 1)], z_recv.at[1])
    total = z2[0].astype(F32)
    for k in range(1, nz):
        total += z2[k].astype(F32)
    zall[me] = (total * (1.0 / ndp)).astype(BF16)
    each_in_plane(lambda to, dev: send(zall.at[me], zall.at[me], z_send.at[2], z_recv.at[2], dev))

    f = dot(inv_hi, pt[...]) + dot(inv_lo, pt[...])
    f_hi, f_lo = split(f)
    up_hi, up_lo = split(inv.T)
    pg_hi, pg_lo = split(dot(up_hi, f_hi) + dot(up_hi, f_lo) + dot(up_lo, f_hi))
    ft[...] = jnp.concatenate([pg_hi, pg_lo], axis=0).T

    ctx_rows(FAR, xo)

    await_bytes(zall.at[pl.ds(0, nplane - 1)], z_recv.at[2])
    for k in range(nplane):
        zq[(k % ny) * zr : (k % ny + 1) * zr, (k // ny) * zc : (k // ny + 1) * zc] = zall[k]

    await_bytes(yg.at[pl.ds(0, 7)], y_send)
    await_bytes(og.at[pl.ds(0, 7 * rows)], o_send)
    await_bytes(prx.at[pl.ds(0, ndp - 1)], p_send.at[0])
    await_bytes(pall.at[pl.ds(0, ndp - 1)], p_send.at[1])
    await_bytes(gx1.at[0], g_send.at[0])
    await_bytes(gx2.at[pl.ds(0, NX - 1)], g_send.at[1])
    await_bytes(z1.at[pl.ds(0, nplane - 1)], z_send.at[0])
    await_bytes(z2.at[pl.ds(0, nz - 1)], z_send.at[1])
    await_bytes(zall.at[pl.ds(0, nplane - 1)], z_send.at[2])


def finish(cs, gb, ev, ft, lf, zq, dctx_hbm, ne_hbm, qf_hbm, ns, qo, store):
    outs = []

    def put(src, dst):
        out = pltpu.make_async_copy(src, dst, store.at[len(outs)])
        out.start()
        outs.append(out)

    part = cs.shape[0] // 4
    for i in range(4):
        put(cs.at[pl.ds(i * part, part)], dctx_hbm.at[pl.ds(i * part, part)])
    zz = jnp.concatenate([zq[...], zq[...]], axis=0)
    step = ns.shape[0] // 4
    for i in range(4):
        r = pl.ds(i * step, step)
        low = dot(ft[r, :], zz)
        ns[r, :] = (gb[r, :].astype(F32) + ev[r, :].astype(F32) - low).astype(BF16)
        put(ns.at[r], ne_hbm.at[0, r])
        if i == 0:
            qo[...] = dot(lf[...], zz)
            put(qo, qf_hbm)
    for out in outs:
        out.wait()


def shards(ny, nz, context, out_grad, out_weight, error, q_init):
    tokens, inner = context.shape
    rows, d = out_grad.shape
    ndp, nplane = ny * nz, 2 * NX * ny
    dma = pltpu.SemaphoreType.DMA
    hbm, in_vmem = pl.BlockSpec(memory_space=pltpu.HBM), pl.BlockSpec(memory_space=pltpu.VMEM)
    pr, pc = RANK // ny, inner // nz
    zr, zc = RANK // ny, d // (2 * NX)
    vm = pltpu.VMEM
    kept = pl.pallas_call(
        functools.partial(kernel, ny, nz),
        out_shape=(
            vm((tokens, inner), BF16),
            vm((inner, d), BF16),
            vm((inner, d), BF16),
            vm((inner, 2 * RANK), BF16),
            vm((RANK, 2 * RANK), BF16),
            vm((RANK, d), BF16),
        ),
        in_specs=[hbm] * 5,
        out_specs=(in_vmem,) * 6,
        scratch_shapes=[
            vm((tokens, inner), BF16),
            vm((inner, tokens), BF16),
            vm((tokens, d), BF16),
            vm((inner, d), BF16),
            vm((d, inner), BF16),
            vm((inner, d), F32),
            vm((RANK, d), F32),
            vm((2 * RANK, d), BF16),
            vm((2 * NX, RANK, rows), BF16),
            vm((RANK, inner), F32),
            vm((ndp, pr, pc), BF16),
            vm((ndp, pr, pc), BF16),
            vm((ndp, pr, pc), BF16),
            vm((RANK, inner), BF16),
            vm((2, RANK // 2, 2 * RANK), F32),
            vm((NX, RANK // 2, 2 * RANK), F32),
            vm((nplane, zr, zc), BF16),
            vm((nplane, zr, zc), BF16),
            vm((nz, zr, zc), BF16),
            vm((nplane, zr, zc), BF16),
            dma((5,)),
            dma, dma, dma,
            dma, dma((2,)), dma((2,)), dma((2,)), dma((5,)),
            dma((2,)), dma((2,)), dma((2,)), dma((2,)), dma((3,)), dma((3,)),
        ],
        compiler_params=pltpu.CompilerParams(
            collective_id=0, has_side_effects=True, vmem_limit_bytes=40 * 2**20
        ),
    )(*(pltpu.with_memory_space_constraint(v, pltpu.HBM) for v in (context, out_grad, out_weight, error, q_init.T)))
    dctx, ne, qf = pl.pallas_call(
        finish,
        out_shape=(
            jax.ShapeDtypeStruct((tokens, inner), BF16),
            jax.ShapeDtypeStruct((1, inner, d), BF16),
            jax.ShapeDtypeStruct((RANK, d), F32),
        ),
        in_specs=[in_vmem] * 6,
        out_specs=(hbm,) * 3,
        scratch_shapes=[vm((inner, d), BF16), vm((RANK, d), F32), dma((9,))],
        compiler_params=pltpu.CompilerParams(vmem_limit_bytes=12 * 2**20),
    )(*kept)
    return dctx, ne, qf.T


def solution(mesh):
    ndp = mesh.shape["dp"]
    ny = 4 if ndp % 4 == 0 else 1
    placed = (
        P("dp", "tensor"),
        P(("dp", "tensor"), None),
        P("tensor", None),
        P("dp", "tensor", None),
        P(),
    )
    return jax.shard_map(
        functools.partial(shards, ny, ndp // ny),
        mesh=mesh,
        in_specs=placed,
        out_specs=(P("dp", "tensor"), P("dp", "tensor", None), P()),
        check_vma=False,
    )
```

```python
import functools

import jax
import jax.numpy as jnp
from jax import lax
from jax.experimental import pallas as pl
from jax.experimental.pallas import tpu as pltpu
from jax.sharding import PartitionSpec as P

MESH = pl.DeviceIdType.MESH
F32 = jnp.float32
BF16 = jnp.bfloat16
NX = 4
RANK = 64
NT = (((1,), (1,)), ((), ()))
NN = (((1,), (0,)), ((), ()))


def dot(a, b, dims=NN):
    return lax.dot_general(a, b, dims, preferred_element_type=F32)


def split(v):
    hi = v.astype(BF16)
    return hi, (v - hi.astype(F32)).astype(BF16)


def eliminate(a):
    row_ids = lax.broadcasted_iota(jnp.int32, a.shape, 0)
    for k in range(0, a.shape[0], 2):
        c0 = jnp.broadcast_to(a[:, k : k + 1], a.shape)
        c1 = jnp.broadcast_to(a[:, k + 1 : k + 2], a.shape)
        r0, r1 = a[k : k + 1, :], a[k + 1 : k + 2, :]
        aa, bb, cc = c0[k : k + 1, :], c0[k + 1 : k + 2, :], c1[k + 1 : k + 2, :]
        inv = 1.0 / (aa * cc - bb * bb)
        w0 = (cc * r0 - bb * r1) * inv
        w1 = (aa * r1 - bb * r0) * inv
        second = r1 - (bb / aa) * r0
        below = a - c0 * w0 - c1 * w1
        a = jnp.where(row_ids > k + 1, below, jnp.where(row_ids == k + 1, second, a))
    return a


def kernel(
    ny, nz,
    ctx_hbm, dy_hbm, w_hbm, e_hbm, q_hbm,
    cs, gb, ev, ft, lf, zq,
    cv, ct, og, wv, wt, acc, qv, q2, yg, pe, ps, prx, pall, pt,
    gx1, gx2, zs, z1, z2, zall,
    load, y_send, y_near, y_sib, o_send, o_left, o_right, o_far, o_sib,
    p_send, p_recv, g_send, g_recv, z_send, z_recv,
):
    dp, ten = lax.axis_index("dp"), lax.axis_index("tensor")
    z, y = dp // ny, dp % ny
    x, core = ten // 2, ten % 2
    ndp, nten = ny * nz, 2 * NX
    nplane = ny * nten
    rows = dy_hbm.shape[0]
    half = rows // 2
    tokens = rows * nten
    inner, d = w_hbm.shape
    xl, xr, xo = lax.rem(x + NX - 1, NX), lax.rem(x + 1, NX), lax.rem(x + 2, NX)
    sib = {"tensor": 2 * x + 1 - core}
    left, right, far = ({"tensor": 2 * i + core} for i in (xl, xr, xo))

    OWN, LEFT, RIGHT, FAR = 0, 1, 2, 3

    def piece(slot, part=None, of=core):
        start = 2 * slot * rows + of * rows
        if part is None:
            return og.at[pl.ds(pl.multiple_of(start, rows), rows)]
        return og.at[pl.ds(pl.multiple_of(start + part * half, half), half)]

    def send(src, dst, s_sem, r_sem, dev):
        pltpu.make_async_remote_copy(
            src_ref=src, dst_ref=dst, send_sem=s_sem, recv_sem=r_sem, device_id=dev, device_id_type=MESH
        ).start()

    def wrap(i, n):
        return jnp.where(i >= n, i - n, i)

    def far_first(n, act):
        act(n // 2)

        @pl.loop(0, n // 2 - 1)
        def _(i):
            act(n // 2 - 1 - i)
            act(n // 2 + 1 + i)

    def each_replica(act):
        def at_z(i):
            to_z = wrap(z + i, nz)
            for j in range(ny):
                to = to_z * ny + wrap(y + j, ny)
                act(to, {"dp": to})

        far_first(nz, at_z)
        for j in range(1, ny):
            to_y = wrap(y + j, ny)
            act(z * ny + to_y, {"dp": z * ny + to_y})

    def each_in_plane(act):
        def at_tensor(i):
            to_t = wrap(ten + i, nten)
            for j in range(ny):
                to_y = wrap(y + j, ny)
                act(to_t * ny + to_y, {"dp": z * ny + to_y, "tensor": to_t})

        far_first(nten, at_tensor)
        for j in range(1, ny):
            to_y = wrap(y + j, ny)
            act(ten * ny + to_y, {"dp": z * ny + to_y})

    def await_bytes(ref, sem):
        pltpu.make_async_copy(ref, ref, sem).wait()

    mine = piece(OWN)
    load_dy = pltpu.make_async_copy(dy_hbm, mine, load.at[0])
    load_q = pltpu.make_async_copy(q_hbm, qv, load.at[1])
    load_e = pltpu.make_async_copy(e_hbm.at[0], ev, load.at[2])
    load_c = pltpu.make_async_copy(ctx_hbm, cv, load.at[3])
    load_w = pltpu.make_async_copy(w_hbm, wv, load.at[4])
    load_q.start()
    load_dy.start()

    barrier = pltpu.get_barrier_semaphore()

    @pl.loop(1, nten)
    def _(j):
        pl.semaphore_signal(barrier, inc=1, device_id={"tensor": jnp.where(ten + j >= nten, ten + j - nten, ten + j)}, device_id_type=MESH)

    @pl.loop(1, ndp)
    def _(j):
        pl.semaphore_signal(barrier, inc=1, device_id={"dp": jnp.where(dp + j >= ndp, dp + j - ndp, dp + j)}, device_id_type=MESH)

    for c in (load_e, load_c, load_w):
        c.start()

    load_q.wait()
    hi, lo = split(qv[...])
    q2[0:RANK] = hi
    q2[RANK : 2 * RANK] = lo
    load_dy.wait()
    yv = dot(q2[...], mine[...], NT)
    yg[ten] = (yv[:RANK] + yv[RANK:]).astype(BF16)

    pl.semaphore_wait(barrier, nten - 1 + ndp - 1)

    for dev in (far, right, left):
        send(yg.at[ten], yg.at[ten], y_send, y_near, dev)
    send(yg.at[ten], yg.at[ten], y_send, y_sib, sib)

    def pass_on(src, dst, sem, dev):
        send(src, dst, o_send, sem, dev)

    for first in (0, 1):
        pass_on(piece(OWN, first), piece(LEFT, first), o_left.at[first], right)
        pass_on(piece(OWN, 1 - first), piece(RIGHT, 1 - first), o_right.at[1 - first], left)
    pass_on(mine, mine, o_sib.at[0], sib)

    def hand_over(slot, part, sem):
        ref = piece(slot, part)
        pass_on(ref, ref, sem, sib)

    def slots(first, count=1):
        return slice(2 * first * rows, 2 * (first + count) * rows)

    mt = inner // 2
    halves = [slice(i * mt, (i + 1) * mt) for i in range(2)]

    def ctx_rows(slot, chip):
        to = pl.ds(pl.multiple_of(2 * chip * rows, 2 * rows), 2 * rows)
        cs[to, :] = dot(og[slots(slot), :], wt[...]).astype(BF16)

    load_e.wait()
    v = dot(q2[...], ev[...], NT)
    pe[...] = v[:RANK] + v[RANK:]
    await_bytes(yg.at[pl.ds(0, 3)], y_near)
    for i in (xl, xr, xo):
        got = yg.at[2 * i + core]
        send(got, got, y_send, y_sib, sib)
    load_c.wait()

    def turn(slot, chip):
        for i in range(2):
            src = pl.ds(pl.multiple_of((2 * chip + i) * rows, rows), rows)
            ct[:, (2 * slot + i) * rows : (2 * slot + i + 1) * rows] = cv[src, :].T

    turn(OWN, x)
    turn(LEFT, xl)
    await_bytes(yg.at[pl.ds(0, 4)], y_sib)

    pv = pe[...] + dot(jnp.concatenate([yg[t] for t in range(nten)], axis=1), cv[...])
    pr, pc = RANK // ny, inner // nz
    pv = pv.astype(BF16)
    for k in range(ndp):
        ps[k] = pv[(k % ny) * pr : (k % ny + 1) * pr, (k // ny) * pc : (k // ny + 1) * pc]

    each_replica(lambda to, dev: send(ps.at[to], prx.at[dp], p_send.at[0], p_recv.at[0], dev))

    prx[dp] = ps[dp]

    turn(RIGHT, xr)
    turn(FAR, xo)
    await_bytes(piece(LEFT, 0), o_left.at[0])
    pass_on(piece(LEFT, 0), piece(FAR, 0), o_far.at[0], right)
    hand_over(LEFT, 0, o_sib.at[1])
    await_bytes(piece(RIGHT, 1), o_right.at[1])
    pass_on(piece(RIGHT, 1), piece(FAR, 1), o_far.at[1], left)
    hand_over(RIGHT, 1, o_sib.at[2])
    load_w.wait()
    wt[...] = wv[...].T
    await_bytes(piece(OWN, of=1 - core), o_sib.at[0])
    ctx_rows(OWN, x)

    await_bytes(prx.at[pl.ds(0, ndp - 1)], p_recv.at[0])
    total = prx[0].astype(F32)
    for k in range(1, ndp):
        total += prx[k].astype(F32)
    pall[dp] = (total * (1.0 / ndp)).astype(BF16)
    each_replica(lambda to, dev: send(pall.at[dp], pall.at[dp], p_send.at[1], p_recv.at[1], dev))

    await_bytes(piece(LEFT, 1), o_left.at[1])
    hand_over(LEFT, 1, o_sib.at[5])
    await_bytes(piece(RIGHT, 0), o_right.at[0])
    hand_over(RIGHT, 0, o_sib.at[6])
    await_bytes(piece(LEFT, 0, 1 - core), o_sib.at[1])
    await_bytes(piece(RIGHT, 1, 1 - core), o_sib.at[2])
    await_bytes(piece(LEFT, 1, 1 - core), o_sib.at[5])
    await_bytes(piece(RIGHT, 0, 1 - core), o_sib.at[6])
    for r in halves:
        v = dot(ct[r, slots(OWN, 3)], og[slots(OWN, 3), :])
        acc[r, :] = v
        gb[r, :] = v.astype(BF16)
    for part in (0, 1):
        await_bytes(piece(FAR, part), o_far.at[part])
        hand_over(FAR, part, o_sib.at[3 + part])

    await_bytes(pall.at[pl.ds(0, ndp - 1)], p_recv.at[1])
    for k in range(ndp):
        pt[(k % ny) * pr : (k % ny + 1) * pr, (k // ny) * pc : (k // ny + 1) * pc] = pall[k]
    zv = dot(pt[...], ev[...]) + dot(pt[...], gb[...])
    met = dot(pt[...], ct[:, slots(FAR)]).astype(BF16)
    for part in (0, 1):
        await_bytes(piece(FAR, part, 1 - core), o_sib.at[3 + part])
    zv = (zv + dot(met, og[slots(FAR), :])).astype(BF16)
    zr, zc = RANK // ny, d // nten
    for k in range(nplane):
        zs[k] = zv[(k % ny) * zr : (k % ny + 1) * zr, (k // ny) * zc : (k // ny + 1) * zc]
    me = ten * ny + y
    each_in_plane(lambda to, dev: send(zs.at[to], z1.at[me], z_send.at[0], z_recv.at[0], dev))
    z1[me] = zs[me]

    gram = dot(pt[...], pt[...], NT)
    gx1[core] = jnp.concatenate([gram[: RANK // 2], gram[RANK // 2 :]], axis=1)
    send(gx1.at[core], gx1.at[core], g_send.at[0], g_recv.at[0], sib)

    def last_rows(r):
        gb[r, :] = (acc[r, :] + dot(ct[r, slots(FAR)], og[slots(FAR), :])).astype(BF16)

    last_rows(halves[0])
    await_bytes(gx1.at[0], g_recv.at[0])
    gx2[x] = gx1[0] + gx1[1]
    for dev in (far, right, left):
        send(gx2.at[x], gx2.at[x], g_send.at[1], g_recv.at[1], dev)
    last_rows(halves[1])
    ctx_rows(LEFT, xl)

    await_bytes(z1.at[pl.ds(0, nplane - 1)], z_recv.at[0])
    total = z1[0].astype(F32)
    for k in range(1, nplane):
        total += z1[k].astype(F32)
    z2[z] = total.astype(BF16)

    far_first(nz, lambda i: send(z2.at[z], z2.at[z], z_send.at[1], z_recv.at[1], {"dp": wrap(z + i, nz) * ny + y}))

    await_bytes(gx2.at[pl.ds(0, NX - 1)], g_recv.at[1])
    gram = gx2[0] + gx2[1] + gx2[2] + gx2[3]
    gram = jnp.concatenate([gram[:, :RANK], gram[:, RANK:]], axis=0)
    on_diag = lax.broadcasted_iota(jnp.int32, (RANK, RANK), 0) == lax.broadcasted_iota(jnp.int32, (RANK, RANK), 1)
    diag = jnp.where(on_diag, gram, 0.0)
    scale = 1.0 / jnp.sqrt(jnp.sum(diag, axis=1, keepdims=True))
    across = 1.0 / jnp.sqrt(jnp.sum(diag, axis=0, keepdims=True))
    gram = jnp.where(on_diag, 1.0, gram * scale * across)
    a = eliminate(jnp.concatenate([gram, jnp.where(on_diag, across, 0.0)], axis=1))
    diag = jnp.sum(jnp.where(on_diag, a[:, :RANK], 0.0), axis=1, keepdims=True)
    inv = a[:, RANK:] / jnp.sqrt(diag)
    inv_hi, inv_lo = split(inv)
    lf[...] = jnp.concatenate([inv_hi, inv_lo], axis=1)

    await_bytes(z2.at[pl.ds(0, nz - 1)], z_recv.at[1])
    total = z2[0].astype(F32)
    for k in range(1, nz):
        total += z2[k].astype(F32)
    zall[me] = (total * (1.0 / ndp)).astype(BF16)
    each_in_plane(lambda to, dev: send(zall.at[me], zall.at[me], z_send.at[2], z_recv.at[2], dev))

    f = dot(inv_hi, pt[...]) + dot(inv_lo, pt[...])
    f_hi, f_lo = split(f)
    up_hi, up_lo = split(inv.T)
    pg_hi, pg_lo = split(dot(up_hi, f_hi) + dot(up_hi, f_lo) + dot(up_lo, f_hi))
    ft[...] = jnp.concatenate([pg_hi, pg_lo], axis=0).T

    ctx_rows(RIGHT, xr)
    ctx_rows(FAR, xo)

    await_bytes(zall.at[pl.ds(0, nplane - 1)], z_recv.at[2])
    for k in range(nplane):
        zq[(k % ny) * zr : (k % ny + 1) * zr, (k // ny) * zc : (k // ny + 1) * zc] = zall[k]

    await_bytes(yg.at[pl.ds(0, 7)], y_send)
    await_bytes(og.at[pl.ds(0, 7 * rows)], o_send)
    await_bytes(prx.at[pl.ds(0, ndp - 1)], p_send.at[0])
    await_bytes(pall.at[pl.ds(0, ndp - 1)], p_send.at[1])
    await_bytes(gx1.at[0], g_send.at[0])
    await_bytes(gx2.at[pl.ds(0, NX - 1)], g_send.at[1])
    await_bytes(z1.at[pl.ds(0, nplane - 1)], z_send.at[0])
    await_bytes(z2.at[pl.ds(0, nz - 1)], z_send.at[1])
    await_bytes(zall.at[pl.ds(0, nplane - 1)], z_send.at[2])


def finish(cs, gb, ev, ft, lf, zq, dctx_hbm, ne_hbm, qf_hbm, ns, qo, store):
    outs = []

    def put(src, dst):
        out = pltpu.make_async_copy(src, dst, store.at[len(outs)])
        out.start()
        outs.append(out)

    part = cs.shape[0] // 4
    for i in range(4):
        put(cs.at[pl.ds(i * part, part)], dctx_hbm.at[pl.ds(i * part, part)])
    zz = jnp.concatenate([zq[...], zq[...]], axis=0)
    step = ns.shape[0] // 4
    for i in range(4):
        r = pl.ds(i * step, step)
        low = dot(ft[r, :], zz)
        ns[r, :] = (gb[r, :].astype(F32) + ev[r, :].astype(F32) - low).astype(BF16)
        put(ns.at[r], ne_hbm.at[0, r])
        if i == 0:
            qo[...] = dot(lf[...], zz)
            put(qo, qf_hbm)
    for out in outs:
        out.wait()


def shards(ny, nz, context, out_grad, out_weight, error, q_init):
    tokens, inner = context.shape
    rows, d = out_grad.shape
    ndp, nplane = ny * nz, 2 * NX * ny
    dma = pltpu.SemaphoreType.DMA
    hbm, in_vmem = pl.BlockSpec(memory_space=pltpu.HBM), pl.BlockSpec(memory_space=pltpu.VMEM)
    pr, pc = RANK // ny, inner // nz
    zr, zc = RANK // ny, d // (2 * NX)
    vm = pltpu.VMEM
    kept = pl.pallas_call(
        functools.partial(kernel, ny, nz),
        out_shape=(
            vm((tokens, inner), BF16),
            vm((inner, d), BF16),
            vm((inner, d), BF16),
            vm((inner, 2 * RANK), BF16),
            vm((RANK, 2 * RANK), BF16),
            vm((RANK, d), BF16),
        ),
        in_specs=[hbm] * 5,
        out_specs=(in_vmem,) * 6,
        scratch_shapes=[
            vm((tokens, inner), BF16),
            vm((inner, tokens), BF16),
            vm((tokens, d), BF16),
            vm((inner, d), BF16),
            vm((d, inner), BF16),
            vm((inner, d), F32),
            vm((RANK, d), F32),
            vm((2 * RANK, d), BF16),
            vm((2 * NX, RANK, rows), BF16),
            vm((RANK, inner), F32),
            vm((ndp, pr, pc), BF16),
            vm((ndp, pr, pc), BF16),
            vm((ndp, pr, pc), BF16),
            vm((RANK, inner), BF16),
            vm((2, RANK // 2, 2 * RANK), F32),
            vm((NX, RANK // 2, 2 * RANK), F32),
            vm((nplane, zr, zc), BF16),
            vm((nplane, zr, zc), BF16),
            vm((nz, zr, zc), BF16),
            vm((nplane, zr, zc), BF16),
            dma((5,)),
            dma, dma, dma,
            dma, dma((2,)), dma((2,)), dma((2,)), dma((7,)),
            dma((2,)), dma((2,)), dma((2,)), dma((2,)), dma((3,)), dma((3,)),
        ],
        compiler_params=pltpu.CompilerParams(
            collective_id=0, has_side_effects=True, vmem_limit_bytes=40 * 2**20
        ),
    )(*(pltpu.with_memory_space_constraint(v, pltpu.HBM) for v in (context, out_grad, out_weight, error, q_init.T)))
    dctx, ne, qf = pl.pallas_call(
        finish,
        out_shape=(
            jax.ShapeDtypeStruct((tokens, inner), BF16),
            jax.ShapeDtypeStruct((1, inner, d), BF16),
            jax.ShapeDtypeStruct((RANK, d), F32),
        ),
        in_specs=[in_vmem] * 6,
        out_specs=(hbm,) * 3,
        scratch_shapes=[vm((inner, d), BF16), vm((RANK, d), F32), dma((9,))],
        compiler_params=pltpu.CompilerParams(vmem_limit_bytes=12 * 2**20),
    )(*kept)
    return dctx, ne, qf.T


def solution(mesh):
    ndp = mesh.shape["dp"]
    ny = 4 if ndp % 4 == 0 else 1
    placed = (
        P("dp", "tensor"),
        P(("dp", "tensor"), None),
        P("tensor", None),
        P("dp", "tensor", None),
        P(),
    )
    return jax.shard_map(
        functools.partial(shards, ny, ndp // ny),
        mesh=mesh,
        in_specs=placed,
        out_specs=(P("dp", "tensor"), P("dp", "tensor", None), P()),
        check_vma=False,
    )
```
